32 devices in a mesh: dp: 4 (over y, x), expert: 8 (over z, core).
Axes of the slice: x: 2, y: 2, z: 4, core: 2. Of those that a mesh axis runs over, the one named last changes fastest.
Arguments:
- tokens: bfloat16 [64, 6144], P('dp'), may hold values from -6 to 6
- w_gate: bfloat16 [6144, 32768], P(None, ('expert', 'dp')), may hold values from -0.078125 to 0.078125
- w_up: bfloat16 [6144, 32768], P(None, ('expert', 'dp')), may hold values from -0.078125 to 0.078125
- basis: bfloat16 [2, 32768, 6144], P(None, ('expert', 'dp')), may hold values from -5 to 5
- routes: int32 [64, 2], replicated, may hold values from 0 to 3, all different within a row; in each aligned block of 16 rows (0 to 15, 16 to 31, ...) at most 9 rows name the same one
- gates: float32 [64, 2], replicated, may hold values from 0.1 to 0.9
- rho: float32 [64], P('dp'), may hold values from 0.3 to 3
- sigma: float32 [6144], replicated, may hold values from 0.3 to 3
Outputs:
- krylov_next: bfloat16 [32768, 6144], P(('expert', 'dp'))
- hessenberg: float32 [3, 1], replicated
The draws below stay inside these ranges and needn't reach their ends.
Inputs may be any that keep to these rules, and one draw needn't show every extreme that they name: `routes`: in each aligned block of 16 rows (the rows of one index of dp), no expert is named by more than 9 rows; the 2 entries of a row differ.
All inputs are finite; a program needn't handle non-finite values.
Results may differ from the reference program's by a relative error of at most 0.0062.
The reference program's roundings to bfloat16 on the way (of `picked`, `hidden` and `cotangent`) count: a program that leaves them out, or rounds other values in their place, can miss the bound.
Values may be sent and summed in bfloat16 or wider, within the bound.
No kernel may reach another device: no remote copies, remote signals or barrier semaphores. Data moves between devices by JAX's collectives and lax.ppermute only.
A program may use at most 192 MiB of HBM per device.

```python
import math
import jax
import jax.numpy as jnp
import numpy as np
from jax import lax

D = 6144
FF = 8192
E = 4
TOP = 2
BASIS = 2
STEPS = 1
TOK_DEV = 16
CAP = 9
TOKENS = 64
N_DP = 4


def draw_basis(key, part):
    common_key = jax.random.fold_in(key, 11)
    own_key = jax.random.fold_in(key, 12)
    common = jax.random.normal(common_key, (1, E * FF, D), jnp.float32)
    own = jax.random.normal(own_key, (BASIS, E * FF, D), jnp.float32)
    return jnp.clip((0.8 * common + own) * 0.78, -5.0, 5.0).astype(jnp.bfloat16)


def block_levels(rng, shape, shards, smallest, largest):
    def one(dim, blocks):
        heights = jax.random.uniform(jax.random.fold_in(jax.random.fold_in(rng, 6), dim), (blocks,), jnp.float32, smallest / len(shards), largest / len(shards))
        return jnp.repeat(jnp.exp(heights), shape[dim] // blocks).reshape((-1,) + (1,) * (len(shape) - dim - 1))

    loudness = one(*shards[0])
    for cut in shards[1:]:
        loudness = loudness * one(*cut)
    return loudness


def shared_out(key, own, number, rows, amount, top, reach, slope):
    order = jax.random.permutation(key, amount)
    heavy_load, usual = load_shares(amount, rows * top, reach, slope, True), load_shares(amount, rows * top, reach, slope, False)
    places = jnp.arange(amount)

    def named(sizes, rotation):
        used = int((sizes > 0).sum())
        fixed = max(1, used // 4)
        moved = fixed + (places - fixed + rotation * (used - fixed)) % max(1, amount - fixed)
        return jnp.zeros((amount,), jnp.int32).at[order[jnp.where(places < fixed, places, moved)]].set(jnp.asarray(sizes, jnp.int32))

    sizes = jnp.where(number % 4 == 0, named(heavy_load, number // 4), named(usual, number - number // 4 - 1))
    mixed = jax.random.permutation(jax.random.fold_in(own, 3), amount)
    giver, sink = mixed[0:amount // 2 * 2:2], mixed[1:amount // 2 * 2:2]
    slack = jnp.minimum(sizes[giver] - 1, reach - sizes[sink]) // 2
    slack = jnp.where((giver == order[0]) | (sink == order[0]) | (sizes[sink] == 0), 0, jnp.maximum(slack, 0))
    moved = jax.random.randint(jax.random.fold_in(own, 4), (amount // 2,), 0, 1 << 20) % (slack + 1)
    sizes = sizes.at[giver].add(-moved).at[sink].add(moved)
    items = jnp.searchsorted(jnp.cumsum(sizes), jnp.arange(rows * top), side="right").astype(jnp.int32)
    grid = items.reshape(top, rows).T
    grid = grid[jax.random.permutation(jax.random.fold_in(own, 1), rows)]
    rotation = jax.random.randint(jax.random.fold_in(own, 2), (rows, 1), 0, top)
    return jnp.take_along_axis(grid, (jnp.arange(top)[None, :] + rotation) % top, axis=1)


def load_shares(count, total, bound, lean, full):
    loads = [(1 << 20) // math.isqrt(rank ** lean) + 1 for rank in range(1, count + 1)]
    largest = bound if full else min(bound, max(-(-total // count), total * loads[0] // sum(loads)))
    least = 1 if total - largest >= count - 1 else 0
    counts, surplus = [largest] + [least] * (count - 1), total - largest - least * (count - 1)
    while surplus > 0:
        candidates = [i for i in range(1, count) if counts[i] < largest] or [i for i in range(1, count) if counts[i] < bound]
        whole, budget = sum([loads[i] for i in candidates]), surplus
        for i in candidates:
            extra = min(bound - counts[i], max(1, budget * loads[i] // whole), surplus)
            counts[i] = counts[i] + extra
            surplus = surplus - extra
    return np.array(counts)


def gaussian(key, extent, deviation, reach, split=(), held_as=jnp.bfloat16):
    result = deviation * jax.random.normal(key, extent, jnp.float32)
    if split:
        result = result * block_levels(key, extent, split, -0.22, 0.18)
    return jnp.clip(result, -reach, reach).astype(held_as)


def setup_inputs(seed: int = 0) -> dict:
    arg_keys = jax.random.split(jax.random.key(seed), 9)
    tokens = gaussian(arg_keys[0], (TOKENS, D), 1.0, 6.0, ((0, 4),))
    w_gate = gaussian(arg_keys[1], (D, E * FF), D ** -0.5, 0.078125, ((1, 32),))
    w_up = gaussian(arg_keys[2], (D, E * FF), D ** -0.5, 0.078125, ((1, 32),))
    basis = draw_basis(jax.random.fold_in(arg_keys[8], 71), 0)
    routes_keys = jax.random.split(jax.random.fold_in(arg_keys[4], 1), TOKENS // TOK_DEV)
    routes_turns = jax.random.permutation(jax.random.fold_in(arg_keys[4], 3), TOKENS // TOK_DEV)
    routes = jax.vmap(lambda own, number: shared_out(jax.random.fold_in(arg_keys[4], 2), own, number, TOK_DEV, E, TOP, CAP, 1))(routes_keys, routes_turns).reshape((TOKENS, TOP))
    gates = jnp.clip(jax.random.uniform(arg_keys[5], (TOKENS, TOP), jnp.float32, 0.1, 0.9), 0.1, 0.9)
    rho = jnp.clip(jnp.exp(math.log(3.0) - 2.3025851 * jax.random.uniform(arg_keys[6], (TOKENS,), jnp.float32) ** block_levels(arg_keys[6], (TOKENS,), ((0, 4),), -0.2, 0.2)), 0.3, 3.0)
    sigma = jnp.clip(jnp.exp(jax.random.uniform(arg_keys[7], (D,), jnp.float32, math.log(0.3), math.log(3.0))), 0.3, 3.0)
    return dict(tokens=tokens, w_gate=w_gate, w_up=w_up, basis=basis, routes=routes, gates=gates, rho=rho, sigma=sigma)


def slot_tables(routes, gates, expert_id, sources, tok_dev, capacity):
    matches = (routes == expert_id).reshape(sources, tok_dev, routes.shape[1])
    member = lax.optimization_barrier(jnp.sum(matches.astype(jnp.int32), axis=2))
    gate_tok = lax.optimization_barrier(jnp.sum(jnp.where(matches, gates.reshape(sources, tok_dev, routes.shape[1]), 0.0), axis=2))
    slot_rank = jnp.cumsum(member, axis=1) - 1
    slot_index = lax.broadcasted_iota(jnp.int32, (sources, capacity, tok_dev), 1)
    placing = jnp.where((slot_rank[:, None, :] == slot_index) & (member[:, None, :] > 0), 1.0, 0.0).astype(jnp.float32)
    slot_gate = lax.optimization_barrier(jnp.sum(placing * gate_tok[:, None, :], axis=2))
    return (placing, slot_gate)

def reference(tokens, w_gate, w_up, basis, routes, gates, rho, sigma):
    scale_back = 1.0 / math.sqrt(FF)
    kappa = E * FF / TOKENS
    entries = float(E * FF * D)
    eye_block = jnp.eye(N_DP, dtype=jnp.float32)
    tables = []
    for expert in range(E):
        placing, slot_gate = slot_tables(routes, gates, expert, N_DP, TOK_DEV, CAP)
        full = (placing[:, :, None, :] * eye_block[:, None, :, None]).reshape(N_DP * CAP, TOKENS)
        picked = jnp.dot(full.astype(jnp.bfloat16), tokens, preferred_element_type=jnp.float32).astype(jnp.bfloat16)
        gate_part = jnp.dot(picked, w_gate[:, expert * FF:(expert + 1) * FF], preferred_element_type=jnp.float32)
        up_part = jnp.dot(picked, w_up[:, expert * FF:(expert + 1) * FF], preferred_element_type=jnp.float32)
        hidden = (jax.nn.silu(gate_part) * up_part * slot_gate.reshape(-1)[:, None]).astype(jnp.bfloat16)
        tables.append((full, hidden))

    def gn_product(direction):
        response = jnp.zeros((TOKENS, D), jnp.float32)
        for expert in range(E):
            full, hidden = tables[expert]
            part = jnp.dot(hidden, direction[expert * FF:(expert + 1) * FF], preferred_element_type=jnp.float32) * scale_back
            response = response + jnp.dot(full.T, part, precision=lax.Precision.HIGHEST)
        cotangent = (kappa * rho[:, None] * sigma[None, :] * response).astype(jnp.bfloat16)
        blocks = []
        for expert in range(E):
            full, hidden = tables[expert]
            chosen = jnp.dot(full.astype(jnp.bfloat16), cotangent, preferred_element_type=jnp.float32).astype(jnp.bfloat16)
            blocks.append(jnp.dot(hidden.T, chosen, preferred_element_type=jnp.float32) * scale_back)
        return jnp.concatenate(blocks, axis=0)
    vectors = [basis[index] for index in range(BASIS)]
    current = basis[BASIS - 1]
    columns = []
    for step in range(STEPS):
        image = gn_product(current)
        coeffs = jnp.stack([jnp.sum(vector.astype(jnp.float32) * image) for vector in vectors]) / entries
        resid = image
        for index in range(len(vectors)):
            resid = resid - coeffs[index] * vectors[index].astype(jnp.float32)
        beta = jnp.sqrt(jnp.sum(resid * resid) / entries)
        current = (resid / beta).astype(jnp.bfloat16)
        padding = jnp.zeros((STEPS - 1 - step,), jnp.float32)
        columns.append(jnp.concatenate([coeffs, padding, beta[None]]))
        vectors.append(current)
    return (current, jnp.stack(columns, axis=1))
```

```python
import functools
import math

import jax
import jax.numpy as jnp
from jax import lax
from jax.experimental import pallas as pl
from jax.experimental.pallas import tpu as pltpu
from jax.sharding import Mesh, PartitionSpec as P

FF = 8192
E = 4
BASIS = 2
STEPS = 1
CAP = 9
MIB = 1 << 20
F32 = jnp.float32
BF16 = jnp.bfloat16
PLANE = ("dp", "slice")
EVERY = ("dp", "group", "slice")


def params(mib=None):
    return pltpu.CompilerParams(vmem_limit_bytes=mib * MIB if mib else None)


def dot(a, b, dims=((1,), (0,))):
    return lax.dot_general(a, b, (dims, ((), ())), preferred_element_type=F32)


def divisor(total, unit, limit):
    best = unit
    for size in range(unit, limit + 1, unit):
        if total % size == 0:
            best = size
    return best


def slot_tables(routes, gates, experts, sources, tok_dev, rows):
    total = sources * tok_dev
    matches = routes[None, :, :] == experts[:, None, None]
    member = jnp.sum(matches.astype(jnp.int32), axis=2)
    gate_tok = jnp.sum(jnp.where(matches, gates[None], 0.0), axis=2)
    token = lax.broadcasted_iota(jnp.int32, (total, total), 0)
    other = lax.broadcasted_iota(jnp.int32, (total, total), 1)
    earlier = (token // tok_dev == other // tok_dev) & (other < token)
    rank = jnp.sum(jnp.where(earlier[None], member[:, None, :], 0), axis=2)
    source = lax.broadcasted_iota(jnp.int32, (1, total), 1) // tok_dev
    slot = jnp.where(member > 0, source * CAP + rank, -1)
    row = lax.broadcasted_iota(jnp.int32, (1, rows, 1), 1)
    placing = (slot[:, None, :] == row).astype(BF16)
    return placing, gate_tok


def hidden_kernel(steps, x_ref, wg_ref, wu_ref, gate_ref, place_ref, out_ref, acc_g, acc_u):
    step = pl.program_id(0)
    x = x_ref[...]
    part_g, part_u = dot(x, wg_ref[...]), dot(x, wu_ref[...])

    @pl.when(step == 0)
    def _():
        acc_g[...] = part_g
        acc_u[...] = part_u

    @pl.when(step > 0)
    def _():
        acc_g[...] += part_g
        acc_u[...] += part_u

    @pl.when(step == steps - 1)
    def _():
        g = acc_g[...]
        full = (g * (1.0 / (1.0 + jnp.exp(-g))) * acc_u[...] * gate_ref[...]).astype(BF16)
        out_ref[...] = dot(place_ref[...], full).astype(BF16)


def hidden_call(x, w_gate, w_up, gate_col, placing):
    tokens, features = x.shape
    units = w_gate.shape[1]
    rows = placing.shape[0]
    depth = divisor(features, 128, 512)
    steps = features // depth
    return pl.pallas_call(
        functools.partial(hidden_kernel, steps),
        grid=(steps,),
        in_specs=[
            pl.BlockSpec((tokens, depth), lambda i: (0, i)),
            pl.BlockSpec((depth, units), lambda i: (i, 0)),
            pl.BlockSpec((depth, units), lambda i: (i, 0)),
            pl.BlockSpec((tokens, 1), lambda i: (0, 0)),
            pl.BlockSpec((rows, tokens), lambda i: (0, 0)),
        ],
        out_specs=pl.BlockSpec((rows, units), lambda i: (0, 0)),
        out_shape=jax.ShapeDtypeStruct((rows, units), BF16),
        scratch_shapes=[pltpu.VMEM((tokens, units), F32)] * 2,
        compiler_params=params(24),
        cost_estimate=pl.CostEstimate(
            flops=4 * tokens * features * units, bytes_accessed=4 * features * units, transcendentals=0
        ),
        name="hidden",
    )(x, w_gate, w_up, gate_col, placing)


def tangent_kernel(scale, place_ref, h_ref, v_ref, out_ref):
    out_ref[0] = (dot(h_ref[...], v_ref[0]) * scale).astype(BF16)


def tangent_call(hidden, basis, index, position, chunks, scale):
    rows, units = hidden.shape
    features = basis.shape[2]
    wide = features // chunks
    return pl.pallas_call(
        functools.partial(tangent_kernel, scale),
        grid_spec=pltpu.PrefetchScalarGridSpec(
            num_scalar_prefetch=1,
            grid=(chunks,),
            in_specs=[
                pl.BlockSpec((rows, units), lambda c, pos: (0, 0)),
                pl.BlockSpec((1, units, wide), lambda c, pos: (index, 0, c)),
            ],
            out_specs=pl.BlockSpec((1, rows, wide), lambda c, pos: (pos[c], 0, 0)),
        ),
        out_shape=jax.ShapeDtypeStruct((chunks, rows, wide), BF16),
        compiler_params=params(16),
        cost_estimate=pl.CostEstimate(
            flops=2 * rows * features * units, bytes_accessed=2 * features * units, transcendentals=0
        ),
        name="tangent",
    )(position, hidden, basis)


def other_kernel(scale, h_ref, v_ref, out_ref, gram_ref, sums):
    step = pl.program_id(0)

    @pl.when(step == 0)
    def _():
        sums[...] = jnp.zeros_like(sums)

    out_ref[0] = (dot(h_ref[...], v_ref[0]) * scale).astype(BF16)
    units = v_ref.shape[1]
    strip = 32 if units % 32 == 0 else units
    wide = v_ref.shape[2]

    def body(i, carry):
        a = v_ref[0, pl.ds(i * strip, strip), :].astype(F32)
        b = v_ref[1, pl.ds(i * strip, strip), :].astype(F32)
        fold = lambda x: jnp.sum(x.reshape(strip // 8, 8, wide), axis=0)
        return carry[0] + fold(a * a), carry[1] + fold(a * b), carry[2] + fold(b * b)

    zero = jnp.zeros((8, wide), F32)
    aa, ab, bb = lax.fori_loop(0, units // strip, body, (zero, zero, zero))
    sums[0] += aa
    sums[1] += ab
    sums[2] += bb

    @pl.when(step == pl.num_programs(0) - 1)
    def _():
        line = lax.broadcasted_iota(jnp.int32, (8, 128), 0)
        gram = jnp.where(line == 3, jnp.sum(sums[0]), 0.0)
        gram = jnp.where(line == 4, jnp.sum(sums[1]), gram)
        gram_ref[...] = jnp.where(line == 5, jnp.sum(sums[2]), gram)


def other_call(hidden, basis, chunks, scale):
    rows, units = hidden.shape
    features = basis.shape[2]
    wide = features // chunks
    return pl.pallas_call(
        functools.partial(other_kernel, scale),
        grid=(chunks,),
        in_specs=[
            pl.BlockSpec((rows, units), lambda c: (0, 0)),
            pl.BlockSpec((BASIS, units, wide), lambda c: (0, 0, c)),
        ],
        out_specs=[
            pl.BlockSpec((1, rows, wide), lambda c: (c, 0, 0)),
            pl.BlockSpec((8, 128), lambda c: (0, 0)),
        ],
        out_shape=[
            jax.ShapeDtypeStruct((chunks, rows, wide), BF16),
            jax.ShapeDtypeStruct((8, 128), F32),
        ],
        scratch_shapes=[pltpu.VMEM((3, 8, wide), F32)],
        compiler_params=params(16),
        cost_estimate=pl.CostEstimate(
            flops=2 * rows * features * units, bytes_accessed=4 * features * units, transcendentals=0
        ),
        name="other_tangent",
    )(hidden, basis)


def pieces(x):
    first = x.astype(BF16)
    rest = x - first.astype(F32)
    second = rest.astype(BF16)
    return first, second, (rest - second.astype(F32)).astype(BF16)


def share_kernel(line, parts, *refs):
    ins, rho_ref, outs = refs[:parts], refs[parts], refs[parts + 1 :]
    rows, wide = ins[0].shape[1:]
    row = lax.broadcasted_iota(jnp.int32, (rows, wide), 0)
    for j, out_ref in enumerate(outs):
        total = ins[0][j].astype(F32)
        for ref in ins[1:]:
            total = total + ref[j].astype(F32)
        if j:
            for n, piece in enumerate(pieces(rho_ref[...])):
                total = jnp.where(row == line + n, piece.astype(F32), total)
        out_ref[...] = total.astype(out_ref.dtype)


def share_call(parts, rho_row, line):
    sources, rows, wide = parts[0].shape
    return pl.pallas_call(
        functools.partial(share_kernel, line, len(parts)),
        out_shape=[jax.ShapeDtypeStruct((rows, wide), BF16 if j else F32) for j in range(sources)],
        compiler_params=params(16),
        name="slice_sum",
    )(*parts, rho_row)


def sum_kernel(line, *refs):
    ins, rho_own, out_ref, rho_ref = refs[:-3], refs[-3], refs[-2], refs[-1]
    total = ins[0][...]
    rho_ref[0:1, :] = rho_own[:, 0:128]
    for j, ref in enumerate(ins[1:]):
        part = ref[...].astype(F32)
        total = total + part
        rho_ref[j + 1 : j + 2, :] = (
            part[line : line + 1, 0:128] + part[line + 1 : line + 2, 0:128] + part[line + 2 : line + 3, 0:128]
        )
    row = lax.broadcasted_iota(jnp.int32, total.shape, 0)
    out_ref[...] = jnp.where(row < line, total, 0.0).astype(BF16)


def sum_call(parts, rho_row, line):
    rows, wide = parts[0].shape
    return pl.pallas_call(
        functools.partial(sum_kernel, line),
        out_shape=[
            jax.ShapeDtypeStruct((rows, wide), BF16),
            jax.ShapeDtypeStruct((len(parts), 128), F32),
        ],
        compiler_params=params(16),
        name="plane_sum",
    )(*parts, rho_row)


def cotangent_kernel(parts, place_ref, rho_ref, sigma_ref, *refs):
    ins, out_ref = refs[:parts], refs[parts]
    response = None
    for j, ref in enumerate(ins):
        term = dot(place_ref[j], ref[...], ((0,), (0,)))
        response = term if response is None else response + term
    cot = (rho_ref[...] * sigma_ref[...] * response).astype(BF16)
    out_ref[...] = dot(place_ref[0], cot).astype(BF16)


def cotangent_call(parts, placing, rho_col, sigma_row):
    return pl.pallas_call(
        functools.partial(cotangent_kernel, len(parts)),
        out_shape=jax.ShapeDtypeStruct(parts[0].shape, BF16),
        compiler_params=params(16),
        name="cotangent",
    )(placing, rho_col, sigma_row, *parts)


def products_kernel(scale, pos_ref, h_ref, c_ref, t0_ref, t1_ref, gram_ref, out_ref):
    chunks, rows, _ = c_ref.shape
    h = h_ref[...]
    weight = dot(h, h, ((1,), (1,)))
    c0 = jnp.zeros(c_ref.shape[1:], F32)
    c1 = jnp.zeros(c_ref.shape[1:], F32)
    square = jnp.zeros((rows, rows), F32)
    for c in range(chunks):
        cot = c_ref[c]
        wide = cot.astype(F32)
        c0 = c0 + wide * t0_ref[c].astype(F32)
        c1 = c1 + wide * t1_ref[pos_ref[c]].astype(F32)
        square = square + dot(cot, cot, ((1,), (1,)))
    line = lax.broadcasted_iota(jnp.int32, (8, 128), 0)
    out = jnp.where(line == 0, jnp.sum(c0), gram_ref[...])
    out = jnp.where(line == 1, jnp.sum(c1), out)
    out_ref[...] = jnp.where(line == 2, jnp.sum(weight * square) * (scale * scale), out)


def products_call(position, hidden, cot, t0, t1, gram, scale):
    vmem = pl.BlockSpec(memory_space=pltpu.VMEM)
    return pl.pallas_call(
        functools.partial(products_kernel, scale),
        in_specs=[pl.BlockSpec(memory_space=pltpu.SMEM)] + [vmem] * 5,
        out_specs=vmem,
        out_shape=jax.ShapeDtypeStruct((8, 128), F32),
        compiler_params=params(16),
        name="products",
    )(position, hidden, cot, t0, t1, gram)


def final_kernel(scale, entries, parts_ref, ht_ref, c_ref, v_ref, out_ref, hess_ref, scalars):
    @pl.when(pl.program_id(0) == 0)
    def _():
        total = jnp.sum(parts_ref[...], axis=0) * (1.0 / entries)
        c0, c1, square = total[0:1], total[1:2], total[2:3]
        g00, g01, g11 = total[3:4], total[4:5], total[5:6]
        norm = square - 2.0 * (c0 * c0 + c1 * c1) + c0 * c0 * g00 + 2.0 * c0 * c1 * g01 + c1 * c1 * g11
        beta = jnp.sqrt(jnp.maximum(norm, square * 2.0**-24))
        line = lax.broadcasted_iota(jnp.int32, (8, 128), 0)
        hess_ref[...] = jnp.where(line == 0, c0, jnp.where(line == 1, c1, beta))
        inverse = 1.0 / beta
        scalars[0] = (c0 * inverse)[0, 0]
        scalars[1] = (c1 * inverse)[0, 0]
        scalars[2] = (scale * inverse)[0, 0]

    a0, a1, s = scalars[0], scalars[1], scalars[2]
    units = ht_ref.shape[0]
    strip = 128 if units % 128 == 0 else units
    cot = c_ref[0]
    for i in range(units // strip):
        at = pl.ds(i * strip, strip)
        image = dot(ht_ref[at, :], cot)
        out = image * s - a0 * v_ref[0, at, :].astype(F32) - a1 * v_ref[1, at, :].astype(F32)
        out_ref[at, :] = out.astype(BF16)


def final_call(parts, hidden_t, cot, basis, scale, entries):
    units, rows = hidden_t.shape
    chunks, _, wide = cot.shape
    return pl.pallas_call(
        functools.partial(final_kernel, scale, entries),
        grid=(chunks,),
        in_specs=[
            pl.BlockSpec(parts.shape, lambda c: (0, 0, 0)),
            pl.BlockSpec((units, rows), lambda c: (0, 0)),
            pl.BlockSpec((1, rows, wide), lambda c: (c, 0, 0)),
            pl.BlockSpec((BASIS, units, wide), lambda c: (0, 0, c)),
        ],
        out_specs=[
            pl.BlockSpec((units, wide), lambda c: (0, c)),
            pl.BlockSpec((8, 128), lambda c: (0, 0)),
        ],
        out_shape=[
            jax.ShapeDtypeStruct((units, chunks * wide), BF16),
            jax.ShapeDtypeStruct((8, 128), F32),
        ],
        scratch_shapes=[pltpu.SMEM((4,), F32)],
        compiler_params=params(32),
        cost_estimate=pl.CostEstimate(
            flops=2 * rows * units * chunks * wide, bytes_accessed=6 * units * chunks * wide, transcendentals=0
        ),
        name="residual",
    )(parts, hidden_t, cot, basis)


def swap(x, axis, distance):
    size = lax.axis_size(axis)
    return lax.ppermute(x, axis, [(i, i ^ distance) for i in range(size)])


def body(tokens, w_gate, w_up, basis, routes, gates, rho, sigma):
    sources, slices = lax.axis_size("dp"), lax.axis_size("slice")
    source, group, part = lax.axis_index("dp"), lax.axis_index("group"), lax.axis_index("slice")
    tok_dev, features = tokens.shape
    total = tok_dev * sources
    scale = 1.0 / math.sqrt(FF)
    kappa = E * FF / total
    entries = float(E * FF * features)
    line = sources * CAP
    rows = -(-(line + 3) // 8) * 8
    split = features % (slices * sources * 128) == 0
    cuts = slices if split else 1
    chunks = sources * cuts
    wide = features // chunks
    column = lax.broadcasted_iota(jnp.int32, (chunks,), 0)
    position = ((column % cuts) ^ (part if split else 0)) * sources + ((column // cuts) ^ source)
    own = source * cuts + (part if split else 0)

    placing, gate_tok = slot_tables(
        routes, gates, group ^ jnp.arange(E, dtype=jnp.int32), sources, tok_dev, rows
    )
    w_gate, w_up, basis = (pltpu.with_memory_space_constraint(x, pltpu.HBM) for x in (w_gate, w_up, basis))
    everyone = lax.all_gather(tokens, "dp", axis=0, tiled=True)
    hidden = hidden_call(everyone, w_gate, w_up, gate_tok[0][:, None], placing[0])

    t1 = tangent_call(hidden, basis, BASIS - 1, position, chunks, scale)
    by_slice = t1.reshape(cuts, sources, rows, wide)
    if split:
        got = [by_slice[0]] + [swap(by_slice[j], "slice", j) for j in range(1, slices)]
    else:
        got = [lax.psum(by_slice[0].astype(F32), "slice")]
    rho_row = jnp.pad(rho[None, :], ((0, 0), (0, wide - tok_dev)))
    shares = share_call(got, rho_row, line)
    got = [shares[0]] + [swap(shares[j], "dp", j) for j in range(1, sources)]
    t0, gram = other_call(hidden, basis, chunks, scale)
    summed, rho_all = sum_call(got, rho_row, line)
    got = [summed] + [swap(summed, "group", j) for j in range(1, E)]
    order = source ^ jnp.arange(sources, dtype=jnp.int32)
    pick = order[:, None] == jnp.arange(sources, dtype=jnp.int32)[None, :]
    rho_all = jnp.sum(jnp.where(pick[:, :, None], rho_all[None, :, :tok_dev], 0.0), axis=1)
    rho_col = (kappa * rho_all).reshape(total, 1)
    sigma_row = lax.dynamic_index_in_dim(sigma.reshape(chunks, wide), own, 0, keepdims=True)
    cot = cotangent_call(got, placing, rho_col, sigma_row)
    cot = lax.all_gather(cot, PLANE if split else "dp", axis=0)

    sums = products_call(position, hidden, cot, t0, t1, gram, scale)
    devices = sources * E * slices
    sums = lax.all_to_all(jnp.broadcast_to(sums, (devices, 8, 128)), EVERY, 0, 0, tiled=True)
    new, hess = final_call(sums, hidden.T, cot, basis, scale, entries)
    return new, hess[: BASIS + 1, :1]


def solution(mesh):
    sources, experts = mesh.shape["dp"], mesh.shape["expert"]
    fine = Mesh(mesh.devices.reshape(sources, E, experts // E), EVERY)
    units = ("group", "slice", "dp")
    return jax.shard_map(
        body,
        mesh=fine,
        in_specs=(
            P("dp", None),
            P(None, units),
            P(None, units),
            P(None, units, None),
            P(),
            P(),
            P("dp"),
            P(),
        ),
        out_specs=(P(units, None), P()),
        check_vma=False,
    )
```

```python
import functools
import math

import jax
import jax.numpy as jnp
from jax import lax
from jax.experimental import pallas as pl
from jax.experimental.pallas import tpu as pltpu
from jax.sharding import Mesh, PartitionSpec as P

FF = 8192
E = 4
BASIS = 2
STEPS = 1
CAP = 9
MIB = 1 << 20
F32 = jnp.float32
BF16 = jnp.bfloat16
PLANE = ("dp", "slice")
EVERY = ("dp", "group", "slice")


def params(mib=None):
    return pltpu.CompilerParams(vmem_limit_bytes=mib * MIB if mib else None)


def pinned(*arrays):
    return tuple(pltpu.with_memory_space_constraint(x, pltpu.VMEM) for x in arrays)


def dot(a, b, dims=((1,), (0,))):
    return lax.dot_general(a, b, (dims, ((), ())), preferred_element_type=F32)


def divisor(total, unit, limit):
    best = unit
    for size in range(unit, limit + 1, unit):
        if total % size == 0:
            best = size
    return best


def load_kernel(tok_dev, ids_ref, routes_ref, gates_ref, rho_ref, sigma_ref, wg_hbm, wu_hbm, *outs):
    wg_ref, wu_ref, place_ref, gate_ref, rho_row_ref, sigma_row_ref, sems = outs
    source, group, chunk = ids_ref[0], ids_ref[1], ids_ref[2]
    blocks = sems.shape[1]
    depth = wg_ref.shape[0] // blocks
    copies = []
    for i in range(blocks):
        at = pl.ds(i * depth, depth)
        copies.append(pltpu.make_async_copy(wg_hbm.at[at], wg_ref.at[at], sems.at[0, i]))
        copies.append(pltpu.make_async_copy(wu_hbm.at[at], wu_ref.at[at], sems.at[1, i]))
    for copy in copies:
        copy.start()

    experts, rows, total = place_ref.shape
    routes, gates = routes_ref[...], gates_ref[...]
    first = lax.broadcasted_iota(jnp.int32, (total, total), 0)
    second = lax.broadcasted_iota(jnp.int32, (total, total), 1)
    earlier = ((first // tok_dev == second // tok_dev) & (first < second)).astype(F32).astype(BF16)
    expert = lax.broadcasted_iota(jnp.int32, (8, total), 0) ^ group
    member = jnp.zeros((8, total), F32)
    for k in range(routes.shape[0]):
        member = member + (routes[k : k + 1, :] == expert).astype(F32)
    rank = dot(member.astype(BF16), earlier).astype(jnp.int32)
    start = (lax.broadcasted_iota(jnp.int32, (8, total), 1) // tok_dev) * CAP
    slot = jnp.where(member > 0.0, start + rank, -1)
    row = lax.broadcasted_iota(jnp.int32, (rows, total), 0)
    places = [(slot[e : e + 1, :] == row).astype(F32).astype(BF16) for e in range(experts)]
    swapped = (first // tok_dev == (second // tok_dev) ^ source) & (first % tok_dev == second % tok_dev)
    for e in range(experts):
        place_ref[e] = dot(places[e], swapped.astype(F32).astype(BF16)).astype(BF16)
    gate = jnp.zeros((1, total), F32)
    for k in range(routes.shape[0]):
        gate = gate + jnp.where(routes[k : k + 1, :] == group, gates[k : k + 1, :], 0.0)
    gate_ref[...] = jnp.sum(jnp.where(swapped, gate, 0.0), axis=1, keepdims=True)
    wide = rho_row_ref.shape[1]
    rho_row_ref[...] = jnp.zeros_like(rho_row_ref)
    rho_row_ref[:, 0:tok_dev] = rho_ref[...]
    sigma_row_ref[...] = sigma_ref[:, pl.ds(pl.multiple_of(chunk * wide, 128), wide)]

    for copy in copies:
        copy.wait()


def load_call(ids, routes, gates, rho, sigma, w_gate, w_up, tok_dev, rows, wide):
    features, units = w_gate.shape
    total = routes.shape[1]
    blocks = features // divisor(features, 128, 1024)
    vmem = pl.BlockSpec(memory_space=pltpu.VMEM)
    hbm = pl.BlockSpec(memory_space=pltpu.HBM)
    return pl.pallas_call(
        functools.partial(load_kernel, tok_dev),
        in_specs=[pl.BlockSpec(memory_space=pltpu.SMEM), vmem, vmem, vmem, vmem, hbm, hbm],
        out_specs=[vmem] * 6,
        out_shape=[
            pltpu.VMEM((features, units), BF16),
            pltpu.VMEM((features, units), BF16),
            jax.ShapeDtypeStruct((E, rows, total), BF16),
            jax.ShapeDtypeStruct((total, 1), F32),
            jax.ShapeDtypeStruct((1, wide), F32),
            jax.ShapeDtypeStruct((1, wide), F32),
        ],
        scratch_shapes=[pltpu.SemaphoreType.DMA((2, blocks))],
        compiler_params=params(3),
        cost_estimate=pl.CostEstimate(flops=0, bytes_accessed=8 * features * units, transcendentals=0),
        name="load",
    )(ids, routes, gates, rho, sigma, w_gate, w_up)


def hidden_kernel(scale, parts, cuts, column_ref, *refs):
    xs, (wg_ref, wu_ref, gate_ref, place_ref, v_hbm) = refs[:parts], refs[parts : parts + 5]
    outs = refs[parts + 5 :]
    h_ref, v_ref, tangents = outs[0], outs[1], outs[2 : 2 + cuts]
    acc_g, acc_u, sems = outs[2 + cuts :]
    units, features = v_ref.shape
    blocks = sems.shape[0]
    copies = []
    for i in range(blocks):
        at = pl.ds(i * (units // blocks), units // blocks)
        copies.append(pltpu.make_async_copy(v_hbm.at[BASIS - 1, at], v_ref.at[at], sems.at[i]))
    for copy in copies:
        copy.start()

    depth = divisor(features, 128, 1024)
    for i in range(features // depth):
        at = pl.ds(i * depth, depth)
        x = jnp.concatenate([ref[:, at] for ref in xs], axis=0)
        part_g, part_u = dot(x, wg_ref[at, :]), dot(x, wu_ref[at, :])
        if i:
            acc_g[...] += part_g
            acc_u[...] += part_u
        else:
            acc_g[...] = part_g
            acc_u[...] = part_u
    g = acc_g[...]
    full = (g * (1.0 / (1.0 + jnp.exp(-g))) * acc_u[...] * gate_ref[...]).astype(BF16)
    h = dot(place_ref[0], full).astype(BF16)
    h_ref[...] = h

    for copy in copies:
        copy.wait()
    wide = tangents[0].shape[2]
    for j, out_ref in enumerate(tangents):
        for d in range(out_ref.shape[0]):
            start = pl.multiple_of(column_ref[j * out_ref.shape[0] + d] * wide, 128)
            out_ref[d] = (dot(h, v_ref[:, pl.ds(start, wide)]) * scale).astype(out_ref.dtype)


def hidden_call(column, xs, wg, wu, gate, place, basis, cuts, scale):
    _, units, features = basis.shape
    _, rows, total = place.shape
    sources = len(xs)
    wide = features // (cuts * sources)
    blocks = 4 if units % 64 == 0 else 1
    vmem = pl.BlockSpec(memory_space=pltpu.VMEM)
    hbm = pl.BlockSpec(memory_space=pltpu.HBM)
    wg, wu = pinned(wg, wu)
    return pl.pallas_call(
        functools.partial(hidden_kernel, scale, sources, cuts),
        in_specs=[pl.BlockSpec(memory_space=pltpu.SMEM)] + [vmem] * (sources + 4) + [hbm],
        out_specs=[vmem] * (2 + cuts),
        out_shape=[
            jax.ShapeDtypeStruct((rows, units), BF16),
            pltpu.VMEM((units, features), BF16),
        ]
        + [jax.ShapeDtypeStruct((sources, rows, wide), BF16 if j else F32) for j in range(cuts)],
        scratch_shapes=[pltpu.VMEM((total, units), F32)] * 2 + [pltpu.SemaphoreType.DMA((blocks,))],
        compiler_params=params(8),
        cost_estimate=pl.CostEstimate(
            flops=6 * rows * features * units, bytes_accessed=6 * features * units, transcendentals=0
        ),
        name="hidden",
    )(column, *xs, wg, wu, gate, place, basis)


def products_of(pairs, reads, units, features):
    strip = 32 if units % 32 == 0 else units
    wide = 256

    def fold(x):
        return jnp.sum(x.reshape(strip // 8, 8, wide), axis=0)

    def column(q, carry):
        across = pl.ds(pl.multiple_of(q * wide, 128), wide)

        def body(i, sums):
            at = pl.ds(pl.multiple_of(i * strip, strip), strip)
            values = [ref[at, across].astype(F32) for ref in reads]
            return tuple(s + fold(values[a] * values[b]) for s, (a, b) in zip(sums, pairs))

        return lax.fori_loop(0, units // strip, body, carry, unroll=4 if units // strip % 4 == 0 else 1)

    zero = jnp.zeros((8, wide), F32)
    return lax.fori_loop(0, features // wide, column, (zero,) * len(pairs))


def other_kernel(scale, h_ref, v_hbm, after_ref, held_ref, v_ref, t_ref, ht_ref, gram_ref, acc, sems):
    units, features = v_ref.shape
    blocks = sems.shape[0]
    depth = units // blocks
    copies = []
    for i in range(blocks):
        at = pl.ds(i * depth, depth)
        copies.append(pltpu.make_async_copy(v_hbm.at[0, at], v_ref.at[at], sems.at[i]))
    for copy in copies:
        copy.start()
    ht_ref[...] = h_ref[...].astype(F32).T.astype(BF16)
    chunks, _, wide = t_ref.shape
    sums = None
    for i in range(blocks):
        at = pl.ds(i * depth, depth)
        copies[i].wait()
        for c in range(chunks):
            across = pl.ds(c * wide, wide)
            part = dot(h_ref[:, at], v_ref[at, across])
            if i:
                part = part + acc[:, across]
            if i < blocks - 1:
                acc[:, across] = part
            else:
                t_ref[c] = (part * scale).astype(BF16)
        (square,) = products_of(((0, 0),), (v_ref.at[at],), depth, features)
        sums = square if sums is None else sums + square
    gram_ref[...] = sums


def other_call(hidden, basis, after, held, chunks, scale):
    rows, units = hidden.shape
    features = basis.shape[2]
    blocks = 4 if units % 512 == 0 else 1
    vmem = pl.BlockSpec(memory_space=pltpu.VMEM)
    hbm = pl.BlockSpec(memory_space=pltpu.HBM)
    return pl.pallas_call(
        functools.partial(other_kernel, scale),
        in_specs=[vmem, hbm, hbm, vmem],
        out_specs=[vmem] * 4,
        out_shape=[
            pltpu.VMEM((units, features), BF16),
            jax.ShapeDtypeStruct((chunks, rows, features // chunks), BF16),
            jax.ShapeDtypeStruct((units, rows), BF16),
            jax.ShapeDtypeStruct((8, 256), F32),
        ],
        scratch_shapes=[pltpu.VMEM((rows, features), F32), pltpu.SemaphoreType.DMA((blocks,))],
        compiler_params=params(5),
        cost_estimate=pl.CostEstimate(
            flops=2 * rows * features * units, bytes_accessed=2 * features * units, transcendentals=0
        ),
        name="other_tangent",
    )(hidden, basis, after, *pinned(held))


def gram_kernel(v0_ref, v1_ref, after_ref, out_ref):
    units, features = v0_ref.shape
    out_ref[0], out_ref[1] = products_of(((0, 1), (1, 1)), (v0_ref, v1_ref), units, features)


def gram_call(v0, v1, after):
    vmem = pl.BlockSpec(memory_space=pltpu.VMEM)
    v0, v1 = pinned(v0, v1)
    return pl.pallas_call(
        gram_kernel,
        in_specs=[vmem, vmem, pl.BlockSpec(memory_space=pltpu.HBM)],
        out_specs=vmem,
        out_shape=jax.ShapeDtypeStruct((2, 8, 256), F32),
        compiler_params=params(2),
        cost_estimate=pl.CostEstimate(
            flops=4 * v0.shape[0] * v0.shape[1], bytes_accessed=4 * v0.shape[0] * v0.shape[1], transcendentals=0
        ),
        name="gram",
    )(v0, v1, after)


def pieces(x):
    first = x.astype(BF16)
    rest = x - first.astype(F32)
    second = rest.astype(BF16)
    return first, second, (rest - second.astype(F32)).astype(BF16)


def share_kernel(line, parts, *refs):
    ins, rho_ref, outs = refs[:parts], refs[parts], refs[parts + 2 :]
    rows, wide = ins[0].shape[1:]
    row = lax.broadcasted_iota(jnp.int32, (rows, wide), 0)
    for j, out_ref in enumerate(outs):
        total = ins[0][j].astype(F32)
        for ref in ins[1:]:
            total = total + ref[j].astype(F32)
        if j:
            for n, piece in enumerate(pieces(rho_ref[...])):
                total = jnp.where(row == line + n, piece.astype(F32), total)
        out_ref[...] = total.astype(out_ref.dtype)


def share_call(parts, rho_row, line, held):
    sources, rows, wide = parts[0].shape
    return pl.pallas_call(
        functools.partial(share_kernel, line, len(parts)),
        in_specs=[pl.BlockSpec(memory_space=pltpu.VMEM)] * (len(parts) + 2),
        out_shape=[jax.ShapeDtypeStruct((rows, wide), BF16 if j else F32) for j in range(sources)],
        compiler_params=params(6),
        name="slice_sum",
    )(*parts, rho_row, *pinned(held))


def sum_kernel(line, *refs):
    ins, rho_own, out_ref, rho_ref = refs[:-5], refs[-5], refs[-2], refs[-1]
    total = ins[0][...]
    rho_ref[0:1, :] = rho_own[:, 0:128]
    for j, ref in enumerate(ins[1:]):
        part = ref[...].astype(F32)
        total = total + part
        rho_ref[j + 1 : j + 2, :] = (
            part[line : line + 1, 0:128] + part[line + 1 : line + 2, 0:128] + part[line + 2 : line + 3, 0:128]
        )
    row = lax.broadcasted_iota(jnp.int32, total.shape, 0)
    out_ref[...] = jnp.where(row < line, total, 0.0).astype(BF16)


def sum_call(parts, rho_row, line, held):
    rows, wide = parts[0].shape
    return pl.pallas_call(
        functools.partial(sum_kernel, line),
        in_specs=[pl.BlockSpec(memory_space=pltpu.VMEM)] * (len(parts) + 3),
        out_shape=[
            jax.ShapeDtypeStruct((rows, wide), BF16),
            jax.ShapeDtypeStruct((len(parts), 128), F32),
        ],
        compiler_params=params(6),
        name="plane_sum",
    )(*parts, rho_row, *pinned(*held))


def cotangent_kernel(parts, kappa, place_ref, rho_ref, sigma_ref, *refs):
    ins, out_ref = refs[:parts], refs[-1]
    response = None
    for j, ref in enumerate(ins):
        term = dot(place_ref[j], ref[...], ((0,), (0,)))
        response = term if response is None else response + term
    sources, tok_dev = rho_ref.shape[0], response.shape[0] // rho_ref.shape[0]
    down = lax.broadcasted_iota(jnp.int32, (tok_dev, 128), 0)
    across = lax.broadcasted_iota(jnp.int32, (tok_dev, 128), 1)
    columns = [
        jnp.sum(jnp.where(down == across, rho_ref[j : j + 1, :], 0.0), axis=1, keepdims=True)
        for j in range(sources)
    ]
    rho = jnp.concatenate(columns, axis=0)
    cot = (kappa * rho * sigma_ref[...] * response).astype(BF16)
    out_ref[...] = dot(place_ref[0], cot).astype(BF16)


def cotangent_call(parts, placing, rho_all, sigma_row, kappa, held):
    return pl.pallas_call(
        functools.partial(cotangent_kernel, len(parts), kappa),
        in_specs=[pl.BlockSpec(memory_space=pltpu.VMEM)] * (len(parts) + 5),
        out_shape=jax.ShapeDtypeStruct(parts[0].shape, BF16),
        compiler_params=params(6),
        name="cotangent",
    )(placing, rho_all, sigma_row, *parts, *pinned(*held))


def products_kernel(scale, column_ref, h_ref, c_ref, t0_ref, square_ref, gram_ref, *refs):
    tangents, out_ref = refs[:-1], refs[-1]
    rows = c_ref.shape[1]
    h = h_ref[...]
    weight = dot(h, h, ((1,), (1,)))
    c0 = jnp.zeros(c_ref.shape[1:], F32)
    c1 = jnp.zeros(c_ref.shape[1:], F32)
    square = jnp.zeros((rows, rows), F32)
    place = 0
    for t_ref in tangents:
        for d in range(t_ref.shape[0]):
            c = column_ref[place]
            place += 1
            cot = c_ref[c]
            wide = cot.astype(F32)
            c0 = c0 + wide * t0_ref[c].astype(F32)
            c1 = c1 + wide * t_ref[d].astype(F32)
            square = square + dot(cot, cot, ((1,), (1,)))
    values = (
        jnp.sum(c0),
        jnp.sum(c1),
        jnp.sum(weight * square) * (scale * scale),
        jnp.sum(square_ref[...]),
        jnp.sum(gram_ref[0]),
        jnp.sum(gram_ref[1]),
    )
    lane = lax.broadcasted_iota(jnp.int32, out_ref.shape, 2)
    out = jnp.zeros(out_ref.shape, F32)
    for n, value in enumerate(values):
        out = jnp.where(lane == n, value, out)
    out_ref[...] = out


def products_call(column, hidden, cot, t0, square, gram, tangents, scale, devices, held):
    vmem = pl.BlockSpec(memory_space=pltpu.VMEM)
    return pl.pallas_call(
        functools.partial(products_kernel, scale),
        in_specs=[pl.BlockSpec(memory_space=pltpu.SMEM)] + [vmem] * (5 + len(tangents) + len(held)),
        out_specs=vmem,
        out_shape=jax.ShapeDtypeStruct((devices, 1, 128), F32),
        compiler_params=params(8),
        name="products",
    )(column, hidden, cot, t0, square, gram, *tangents, *pinned(*held))


def final_kernel(scale, entries, parts_ref, ht_ref, c_ref, v0_ref, v1_ref, out_ref, hess_ref, scalars):
    units, wide = out_ref.shape

    @pl.when(pl.program_id(0) == 0)
    def _():
        total = jnp.sum(parts_ref[...], axis=0) * (1.0 / entries)
        c0, c1, square = total[:, 0:1], total[:, 1:2], total[:, 2:3]
        g00, g01, g11 = total[:, 3:4], total[:, 4:5], total[:, 5:6]
        norm = square - 2.0 * (c0 * c0 + c1 * c1) + c0 * c0 * g00 + 2.0 * c0 * c1 * g01 + c1 * c1 * g11
        beta = jnp.sqrt(jnp.maximum(norm, square * 2.0**-24))
        line = lax.broadcasted_iota(jnp.int32, (8, 128), 0)
        hess_ref[...] = jnp.where(line == 0, c0, jnp.where(line == 1, c1, beta))
        inverse = 1.0 / beta
        scalars[0] = (c0 * inverse)[0, 0]
        scalars[1] = (c1 * inverse)[0, 0]
        scalars[2] = (scale * inverse)[0, 0]

    a0, a1, s = scalars[0], scalars[1], scalars[2]
    strip = 256 if units % 256 == 0 else units
    across = divisor(wide, 128, 256)
    begin = pl.program_id(0) * wide
    for q in range(wide // across):
        source = pl.ds(pl.multiple_of(begin + q * across, 128), across)
        target = pl.ds(q * across, across)
        cot = c_ref[0, :, target]
        for i in range(units // strip):
            at = pl.ds(i * strip, strip)
            image = dot(ht_ref[at, :], cot)
            out = image * s - a0 * v0_ref[at, source].astype(F32) - a1 * v1_ref[at, source].astype(F32)
            out_ref[at, target] = out.astype(BF16)


def final_call(parts, hidden_t, cot, v0, v1, scale, entries):
    units, rows = hidden_t.shape
    chunks, _, wide = cot.shape
    vmem = pl.BlockSpec(memory_space=pltpu.VMEM)
    v0, v1 = pinned(v0, v1)
    return pl.pallas_call(
        functools.partial(final_kernel, scale, entries),
        grid=(chunks,),
        in_specs=[
            pl.BlockSpec(parts.shape, lambda c: (0, 0, 0)),
            pl.BlockSpec((units, rows), lambda c: (0, 0)),
            pl.BlockSpec((1, rows, wide), lambda c: (c, 0, 0)),
            vmem,
            vmem,
        ],
        out_specs=[
            pl.BlockSpec((units, wide), lambda c: (0, c)),
            pl.BlockSpec((8, 128), lambda c: (0, 0)),
        ],
        out_shape=[
            jax.ShapeDtypeStruct((units, chunks * wide), BF16),
            jax.ShapeDtypeStruct((8, 128), F32),
        ],
        scratch_shapes=[pltpu.SMEM((4,), F32)],
        compiler_params=params(8),
        cost_estimate=pl.CostEstimate(
            flops=2 * rows * units * chunks * wide, bytes_accessed=6 * units * chunks * wide, transcendentals=0
        ),
        name="residual",
    )(parts, hidden_t, cot, v0, v1)


def swap(x, axis, distance):
    size = lax.axis_size(axis)
    return lax.ppermute(x, axis, [(i, i ^ distance) for i in range(size)])


def body(tokens, w_gate, w_up, basis, routes, gates, rho, sigma):
    sources, slices = lax.axis_size("dp"), lax.axis_size("slice")
    source, group, part = lax.axis_index("dp"), lax.axis_index("group"), lax.axis_index("slice")
    tok_dev, features = tokens.shape
    total = tok_dev * sources
    scale = 1.0 / math.sqrt(FF)
    kappa = E * FF / total
    entries = float(E * FF * features)
    line = sources * CAP
    rows = -(-(line + 3) // 8) * 8
    split = features % (slices * sources * 128) == 0
    cuts = slices if split else 1
    chunks = sources * cuts
    wide = features // chunks
    place = jnp.arange(chunks, dtype=jnp.int32)
    lane = part if split else 0
    column = ((place % sources) ^ source) * cuts + ((place // sources) ^ lane)
    ids = jnp.stack([source, group, column[0]]).astype(jnp.int32)
    w_gate, w_up, basis = (pltpu.with_memory_space_constraint(x, pltpu.HBM) for x in (w_gate, w_up, basis))

    xs = [tokens] + [swap(tokens, "dp", j) for j in range(1, sources)]
    wg, wu, placing, gate, rho_row, sigma_row = load_call(
        ids, routes.T, gates.T, rho[None, :], sigma[None, :], w_gate, w_up, tok_dev, rows, wide
    )
    hidden, v1, *tangents = hidden_call(column, xs, wg, wu, gate, placing, basis, cuts, scale)
    if split:
        got = [tangents[0]] + [swap(tangents[j], "slice", j) for j in range(1, slices)]
    else:
        got = [lax.psum(tangents[0], "slice")]
    shares = share_call(got, rho_row, line, v1)
    got = [shares[0]] + [swap(shares[j], "dp", j) for j in range(1, sources)]
    v0, t0, hidden_t, square = other_call(hidden, basis, shares[0], v1, chunks, scale)
    summed, rho_all = sum_call(got, rho_row, line, (v0, v1))
    got = [summed] + [swap(summed, "group", j) for j in range(1, E)]
    gram = gram_call(v0, v1, rho_all)
    cot = cotangent_call(got, placing, rho_all, sigma_row, kappa, (v0, v1))
    cot = lax.all_gather(cot, PLANE if split else "dp", axis=0)

    devices = sources * E * slices
    parts = products_call(column, hidden, cot, t0, square, gram, tangents, scale, devices, ())
    parts = lax.all_to_all(parts, EVERY, 0, 0, tiled=True)
    new, hess = final_call(parts, hidden_t, cot, v0, v1, scale, entries)
    return new, hess[: BASIS + 1, :1]


def solution(mesh):
    sources, experts = mesh.shape["dp"], mesh.shape["expert"]
    fine = Mesh(mesh.devices.reshape(sources, E, experts // E), EVERY)
    units = ("group", "slice", "dp")
    return jax.shard_map(
        body,
        mesh=fine,
        in_specs=(
            P("dp", None),
            P(None, units),
            P(None, units),
            P(None, units, None),
            P(),
            P(),
            P("dp"),
            P(),
        ),
        out_specs=(P(units, None), P()),
        check_vma=False,
    )
```

```python
import functools
import math

import jax
import jax.numpy as jnp
from jax import lax
from jax.experimental import pallas as pl
from jax.experimental.pallas import tpu as pltpu
from jax.sharding import Mesh, PartitionSpec as P

FF = 8192
E = 4
BASIS = 2
STEPS = 1
CAP = 9
MIB = 1 << 20
F32 = jnp.float32
BF16 = jnp.bfloat16
EVERY = ("dp", "group", "slice")


def params(mib=None):
    return pltpu.CompilerParams(vmem_limit_bytes=mib * MIB if mib else None)


def pinned(*arrays):
    return tuple(pltpu.with_memory_space_constraint(x, pltpu.VMEM) for x in arrays)


def dot(a, b, dims=((1,), (0,))):
    return lax.dot_general(a, b, (dims, ((), ())), preferred_element_type=F32)


def divisor(total, unit, limit):
    best = unit
    for size in range(unit, limit + 1, unit):
        if total % size == 0:
            best = size
    return best


def load_kernel(tok_dev, ids_ref, routes_hbm, gates_hbm, rho_hbm, sigma_hbm, wg_hbm, wu_hbm, *outs):
    wg_ref, wu_ref, place_ref, gate_ref, rho_row_ref, sigma_row_ref = outs[:6]
    routes_ref, gates_ref, rho_ref, small_sems, w_sems = outs[6:]
    source, group, chunk = ids_ref[0], ids_ref[1], ids_ref[2]
    wide = rho_row_ref.shape[1]
    here = pl.ds(pl.multiple_of(chunk * wide, 128), wide)
    small = [
        pltpu.make_async_copy(routes_hbm, routes_ref, small_sems.at[0]),
        pltpu.make_async_copy(gates_hbm, gates_ref, small_sems.at[1]),
        pltpu.make_async_copy(rho_hbm, rho_ref, small_sems.at[2]),
        pltpu.make_async_copy(sigma_hbm.at[:, here], sigma_row_ref, small_sems.at[3]),
    ]
    depth = wg_ref.shape[0] // w_sems.shape[1]
    weights = []
    for i in range(w_sems.shape[1]):
        at = pl.ds(i * depth, depth)
        weights.append(pltpu.make_async_copy(wg_hbm.at[at], wg_ref.at[at], w_sems.at[0, i]))
        weights.append(pltpu.make_async_copy(wu_hbm.at[at], wu_ref.at[at], w_sems.at[1, i]))
    for copy in small + weights:
        copy.start()
    for copy in small:
        copy.wait()

    experts, rows, total = place_ref.shape
    routes, gates = routes_ref[...], gates_ref[...]
    first = lax.broadcasted_iota(jnp.int32, (total, total), 0)
    second = lax.broadcasted_iota(jnp.int32, (total, total), 1)
    earlier = ((first // tok_dev == second // tok_dev) & (first < second)).astype(F32).astype(BF16)
    expert = lax.broadcasted_iota(jnp.int32, (8, total), 0) ^ group
    member = jnp.zeros((8, total), F32)
    for k in range(routes.shape[0]):
        member = member + (routes[k : k + 1, :] == expert).astype(F32)
    rank = dot(member.astype(BF16), earlier).astype(jnp.int32)
    start = (lax.broadcasted_iota(jnp.int32, (8, total), 1) // tok_dev) * CAP
    slot = jnp.where(member > 0.0, start + rank, -1)
    row = lax.broadcasted_iota(jnp.int32, (rows, total), 0)
    swapped = (first // tok_dev == (second // tok_dev) ^ source) & (first % tok_dev == second % tok_dev)
    for e in range(experts):
        place = (slot[e : e + 1, :] == row).astype(F32).astype(BF16)
        place_ref[e] = dot(place, swapped.astype(F32).astype(BF16)).astype(BF16)
    gate = jnp.zeros((1, total), F32)
    for k in range(routes.shape[0]):
        gate = gate + jnp.where(routes[k : k + 1, :] == group, gates[k : k + 1, :], 0.0)
    gate_ref[...] = jnp.sum(jnp.where(swapped, gate, 0.0), axis=1, keepdims=True)
    rho_row_ref[...] = jnp.zeros_like(rho_row_ref)
    rho_row_ref[:, 0:tok_dev] = rho_ref[...]

    for copy in weights:
        copy.wait()


def load_call(ids, routes, gates, rho, sigma, w_gate, w_up, tok_dev, rows, wide):
    features, units = w_gate.shape
    total = routes.shape[1]
    vmem = pl.BlockSpec(memory_space=pltpu.VMEM)
    hbm = pl.BlockSpec(memory_space=pltpu.HBM)
    return pl.pallas_call(
        functools.partial(load_kernel, tok_dev),
        in_specs=[pl.BlockSpec(memory_space=pltpu.SMEM)] + [hbm] * 6,
        out_specs=[vmem] * 6,
        out_shape=[
            pltpu.VMEM((features, units), BF16),
            pltpu.VMEM((features, units), BF16),
            jax.ShapeDtypeStruct((E, rows, total), BF16),
            jax.ShapeDtypeStruct((total, 1), F32),
            jax.ShapeDtypeStruct((1, wide), F32),
            jax.ShapeDtypeStruct((1, wide), F32),
        ],
        scratch_shapes=[
            pltpu.VMEM(routes.shape, jnp.int32),
            pltpu.VMEM(gates.shape, F32),
            pltpu.VMEM(rho.shape, F32),
            pltpu.SemaphoreType.DMA((4,)),
            pltpu.SemaphoreType.DMA((2, features // divisor(features, 128, 1024))),
        ],
        compiler_params=params(3),
        cost_estimate=pl.CostEstimate(flops=0, bytes_accessed=8 * features * units, transcendentals=0),
        name="load",
    )(ids, routes, gates, rho, sigma, w_gate, w_up)


def vector_blocks(units):
    return 4 if units % 512 == 0 else 1


def hidden_kernel(scale, parts, cuts, column_ref, *refs):
    xs, (wg_ref, wu_ref, gate_ref, place_ref, v_hbm) = refs[:parts], refs[parts : parts + 5]
    outs = refs[parts + 5 :]
    h_ref, v_ref, tangents = outs[0], outs[1], outs[2 : 2 + cuts]
    acc_g, acc_u, v_sems = outs[2 + cuts :]
    units, features = v_ref.shape
    depth = divisor(features, 128, 1024)
    lots = [pl.ds(i * depth, depth) for i in range(features // depth)]
    height = units // v_sems.shape[0]
    bands = [pl.ds(i * height, height) for i in range(v_sems.shape[0])]
    vectors = [
        pltpu.make_async_copy(v_hbm.at[BASIS - 1, at], v_ref.at[at], v_sems.at[i]) for i, at in enumerate(bands)
    ]
    for copy in vectors:
        copy.start()

    def project(acc, w_ref):
        for i, at in enumerate(lots):
            part = dot(jnp.concatenate([ref[:, at] for ref in xs], axis=0), w_ref[at, :])
            acc[...] = acc[...] + part if i else part

    project(acc_g, wg_ref)
    project(acc_u, wu_ref)
    g = acc_g[...]
    full = (g * (1.0 / (1.0 + jnp.exp(-g))) * acc_u[...] * gate_ref[...]).astype(BF16)
    h_ref[...] = dot(place_ref[0], full).astype(BF16)

    sources, _, wide = tangents[0].shape
    for copy in vectors:
        copy.wait()
    h = h_ref[...]
    for j, out_ref in enumerate(tangents):
        for d in range(sources):
            start = pl.multiple_of(column_ref[j * sources + d] * wide, 128)
            out_ref[d] = (dot(h, v_ref[:, pl.ds(start, wide)]) * scale).astype(out_ref.dtype)


def hidden_call(column, xs, wg, wu, gate, place, basis, cuts, scale):
    _, units, features = basis.shape
    _, rows, total = place.shape
    sources = len(xs)
    wide = features // (cuts * sources)
    vmem = pl.BlockSpec(memory_space=pltpu.VMEM)
    hbm = pl.BlockSpec(memory_space=pltpu.HBM)
    return pl.pallas_call(
        functools.partial(hidden_kernel, scale, sources, cuts),
        in_specs=[pl.BlockSpec(memory_space=pltpu.SMEM)] + [vmem] * (sources + 4) + [hbm],
        out_specs=[vmem] * (2 + cuts),
        out_shape=[
            jax.ShapeDtypeStruct((rows, units), BF16),
            pltpu.VMEM((units, features), BF16),
        ]
        + [jax.ShapeDtypeStruct((sources, rows, wide), BF16 if j else F32) for j in range(cuts)],
        scratch_shapes=[
            pltpu.VMEM((total, units), F32),
            pltpu.VMEM((total, units), F32),
            pltpu.SemaphoreType.DMA((vector_blocks(units),)),
        ],
        compiler_params=params(8),
        cost_estimate=pl.CostEstimate(
            flops=6 * rows * features * units, bytes_accessed=6 * features * units, transcendentals=0
        ),
        name="hidden",
    )(column, *xs, *pinned(wg, wu), gate, place, basis)


def products_of(pairs, reads, units, features):
    strip = 32 if units % 32 == 0 else units
    wide = 256

    def fold(x):
        return jnp.sum(x.reshape(strip // 8, 8, wide), axis=0)

    def column(q, carry):
        across = pl.ds(pl.multiple_of(q * wide, 128), wide)

        def body(i, sums):
            at = pl.ds(pl.multiple_of(i * strip, strip), strip)
            values = [ref[at, across].astype(F32) for ref in reads]
            return tuple(s + fold(values[a] * values[b]) for s, (a, b) in zip(sums, pairs))

        return lax.fori_loop(0, units // strip, body, carry, unroll=4 if units // strip % 4 == 0 else 1)

    zero = jnp.zeros((8, wide), F32)
    return lax.fori_loop(0, features // wide, column, (zero,) * len(pairs))


def other_kernel(scale, h_ref, v_hbm, after_ref, held_ref, v_ref, t_ref, ht_ref, gram_ref, acc, sems):
    units, features = v_ref.shape
    blocks = sems.shape[0]
    depth = units // blocks
    copies = []
    for i in range(blocks):
        at = pl.ds(i * depth, depth)
        copies.append(pltpu.make_async_copy(v_hbm.at[0, at], v_ref.at[at], sems.at[i]))
    for copy in copies:
        copy.start()
    ht_ref[...] = h_ref[...].astype(F32).T.astype(BF16)
    chunks, _, wide = t_ref.shape
    sums = None
    for i in range(blocks):
        at = pl.ds(i * depth, depth)
        copies[i].wait()
        for c in range(chunks):
            across = pl.ds(c * wide, wide)
            part = dot(h_ref[:, at], v_ref[at, across])
            if i:
                part = part + acc[:, across]
            if i < blocks - 1:
                acc[:, across] = part
            else:
                t_ref[c] = (part * scale).astype(BF16)
        (square,) = products_of(((0, 0),), (v_ref.at[at],), depth, features)
        sums = square if sums is None else sums + square
    gram_ref[...] = sums


def other_call(hidden, basis, after, held, chunks, scale):
    rows, units = hidden.shape
    features = basis.shape[2]
    blocks = 4 if units % 512 == 0 else 1
    vmem = pl.BlockSpec(memory_space=pltpu.VMEM)
    hbm = pl.BlockSpec(memory_space=pltpu.HBM)
    return pl.pallas_call(
        functools.partial(other_kernel, scale),
        in_specs=[vmem, hbm, hbm, vmem],
        out_specs=[vmem] * 4,
        out_shape=[
            pltpu.VMEM((units, features), BF16),
            jax.ShapeDtypeStruct((chunks, rows, features // chunks), BF16),
            jax.ShapeDtypeStruct((units, rows), BF16),
            jax.ShapeDtypeStruct((8, 256), F32),
        ],
        scratch_shapes=[pltpu.VMEM((rows, features), F32), pltpu.SemaphoreType.DMA((blocks,))],
        compiler_params=params(5),
        cost_estimate=pl.CostEstimate(
            flops=2 * rows * features * units, bytes_accessed=2 * features * units, transcendentals=0
        ),
        name="other_tangent",
    )(hidden, basis, after, *pinned(held))


def gram_kernel(first, last, v0_ref, v1_ref, after_ref, out_ref):
    at = pl.ds(first, last - first)
    reads = (v0_ref.at[at], v1_ref.at[at])
    out_ref[0], out_ref[1] = products_of(((0, 1), (1, 1)), reads, last - first, v0_ref.shape[1])


def gram_call(v0, v1, after, first, last):
    vmem = pl.BlockSpec(memory_space=pltpu.VMEM)
    size = (last - first) * v0.shape[1]
    return pl.pallas_call(
        functools.partial(gram_kernel, first, last),
        in_specs=[vmem, vmem, pl.BlockSpec(memory_space=pltpu.HBM)],
        out_specs=vmem,
        out_shape=jax.ShapeDtypeStruct((2, 8, 256), F32),
        compiler_params=params(2),
        cost_estimate=pl.CostEstimate(flops=4 * size, bytes_accessed=4 * size, transcendentals=0),
        name="gram",
    )(*pinned(v0, v1), after)


def pieces(x):
    first = x.astype(BF16)
    rest = x - first.astype(F32)
    second = rest.astype(BF16)
    return first, second, (rest - second.astype(F32)).astype(BF16)


def share_kernel(line, parts, *refs):
    ins, rho_ref, outs = refs[:parts], refs[parts], refs[parts + 2 :]
    rows, wide = ins[0].shape[1:]
    row = lax.broadcasted_iota(jnp.int32, (rows, wide), 0)
    for j, out_ref in enumerate(outs):
        total = ins[0][j].astype(F32)
        for ref in ins[1:]:
            total = total + ref[j].astype(F32)
        if j:
            for n, piece in enumerate(pieces(rho_ref[...])):
                total = jnp.where(row == line + n, piece.astype(F32), total)
        out_ref[...] = total.astype(out_ref.dtype)


def share_call(parts, rho_row, line, held):
    sources, rows, wide = parts[0].shape
    return pl.pallas_call(
        functools.partial(share_kernel, line, len(parts)),
        in_specs=[pl.BlockSpec(memory_space=pltpu.VMEM)] * (len(parts) + 2),
        out_shape=[jax.ShapeDtypeStruct((rows, wide), BF16 if j else F32) for j in range(sources)],
        compiler_params=params(6),
        name="slice_sum",
    )(*parts, rho_row, *pinned(*held))


def sum_kernel(line, *refs):
    ins, rho_own, out_ref, rho_ref = refs[:-6], refs[-6], refs[-2], refs[-1]
    total = ins[0][...]
    rho_ref[0:1, :] = rho_own[:, 0:128]
    for j, ref in enumerate(ins[1:]):
        part = ref[...].astype(F32)
        total = total + part
        rho_ref[j + 1 : j + 2, :] = (
            part[line : line + 1, 0:128] + part[line + 1 : line + 2, 0:128] + part[line + 2 : line + 3, 0:128]
        )
    row = lax.broadcasted_iota(jnp.int32, total.shape, 0)
    out_ref[...] = jnp.where(row < line, total, 0.0).astype(BF16)


def sum_call(parts, rho_row, line, held, after):
    rows, wide = parts[0].shape
    return pl.pallas_call(
        functools.partial(sum_kernel, line),
        in_specs=[pl.BlockSpec(memory_space=pltpu.VMEM)] * (len(parts) + 4),
        out_shape=[
            jax.ShapeDtypeStruct((rows, wide), BF16),
            jax.ShapeDtypeStruct((len(parts), 128), F32),
        ],
        compiler_params=params(6),
        name="plane_sum",
    )(*parts, rho_row, *pinned(*held), after)


def cotangent_kernel(parts, kappa, place_ref, rho_ref, sigma_ref, *refs):
    ins, out_ref = refs[:parts], refs[-1]
    response = None
    for j, ref in enumerate(ins):
        term = dot(place_ref[j], ref[...], ((0,), (0,)))
        response = term if response is None else response + term
    sources, tok_dev = rho_ref.shape[0], response.shape[0] // rho_ref.shape[0]
    down = lax.broadcasted_iota(jnp.int32, (tok_dev, 128), 0)
    across = lax.broadcasted_iota(jnp.int32, (tok_dev, 128), 1)
    columns = [
        jnp.sum(jnp.where(down == across, rho_ref[j : j + 1, :], 0.0), axis=1, keepdims=True)
        for j in range(sources)
    ]
    rho = jnp.concatenate(columns, axis=0)
    cot = (kappa * rho * sigma_ref[...] * response).astype(BF16)
    out_ref[...] = dot(place_ref[0], cot).astype(BF16)


def cotangent_call(parts, placing, rho_all, sigma_row, kappa, held, after):
    return pl.pallas_call(
        functools.partial(cotangent_kernel, len(parts), kappa),
        in_specs=[pl.BlockSpec(memory_space=pltpu.VMEM)] * (len(parts) + 6),
        out_shape=jax.ShapeDtypeStruct(parts[0].shape, BF16),
        compiler_params=params(6),
        name="cotangent",
    )(placing, rho_all, sigma_row, *parts, *pinned(*held), after)


def stack_kernel(*refs):
    for j, ref in enumerate(refs[:-2]):
        refs[-1][j] = ref[...]


def stack_call(parts, after):
    return pl.pallas_call(
        stack_kernel,
        in_specs=[pl.BlockSpec(memory_space=pltpu.VMEM)] * (len(parts) + 1),
        out_specs=pl.BlockSpec(memory_space=pltpu.VMEM),
        out_shape=jax.ShapeDtypeStruct((len(parts),) + parts[0].shape, parts[0].dtype),
        compiler_params=params(6),
        name="stack",
    )(*parts, after)


def products_kernel(scale, cuts, column_ref, h_ref, t0_ref, square_ref, *refs):
    out_ref = refs[-1]
    cots, tangents, grams = refs[:cuts], refs[cuts : 2 * cuts], refs[2 * cuts : -1]
    sources, rows, wide = cots[0].shape
    h = h_ref[...]
    weight = dot(h, h, ((1,), (1,)))
    c0 = jnp.zeros((rows, wide), F32)
    c1 = jnp.zeros((rows, wide), F32)
    square = jnp.zeros((rows, rows), F32)
    for j in range(cuts):
        for d in range(sources):
            cot = cots[j][d]
            value = cot.astype(F32)
            c0 = c0 + value * t0_ref[column_ref[j * sources + d]].astype(F32)
            c1 = c1 + value * tangents[j][d].astype(F32)
            square = square + dot(cot, cot, ((1,), (1,)))
    values = (
        jnp.sum(c0),
        jnp.sum(c1),
        jnp.sum(weight * square) * (scale * scale),
        jnp.sum(square_ref[...]),
        jnp.sum(sum(ref[0] for ref in grams)),
        jnp.sum(sum(ref[1] for ref in grams)),
    )
    lane = lax.broadcasted_iota(jnp.int32, out_ref.shape, 2)
    out = jnp.zeros(out_ref.shape, F32)
    for n, value in enumerate(values):
        out = jnp.where(lane == n, value, out)
    out_ref[...] = out


def products_call(column, hidden, t0, square, cots, tangents, grams, scale, devices):
    vmem = pl.BlockSpec(memory_space=pltpu.VMEM)
    args = (hidden, t0, square, *cots, *tangents, *grams)
    return pl.pallas_call(
        functools.partial(products_kernel, scale, len(cots)),
        in_specs=[pl.BlockSpec(memory_space=pltpu.SMEM)] + [vmem] * len(args),
        out_specs=vmem,
        out_shape=jax.ShapeDtypeStruct((devices, 1, 128), F32),
        compiler_params=params(8),
        name="products",
    )(column, *args)


def final_kernel(scale, entries, sources, column_ref, parts_ref, ht_ref, v0_ref, v1_ref, *refs):
    cots, (out_ref, hess_ref, scalars) = refs[:-3], refs[-3:]
    step = pl.program_id(0)

    @pl.when(step == 0)
    def _():
        total = jnp.sum(parts_ref[...], axis=0) * (1.0 / entries)
        c0, c1, square = total[:, 0:1], total[:, 1:2], total[:, 2:3]
        g00, g01, g11 = total[:, 3:4], total[:, 4:5], total[:, 5:6]
        norm = square - 2.0 * (c0 * c0 + c1 * c1) + c0 * c0 * g00 + 2.0 * c0 * c1 * g01 + c1 * c1 * g11
        beta = jnp.sqrt(jnp.maximum(norm, square * 2.0**-24))
        lane = lax.broadcasted_iota(jnp.int32, hess_ref.shape, 1)
        hess_ref[...] = jnp.where(lane == 0, c0, jnp.where(lane == 1, c1, beta))
        inverse = 1.0 / beta
        scalars[0] = (c0 * inverse)[0, 0]
        scalars[1] = (c1 * inverse)[0, 0]
        scalars[2] = (scale * inverse)[0, 0]

    a0, a1, s = scalars[0], scalars[1], scalars[2]
    units, wide = out_ref.shape
    strip = 256 if units % 256 == 0 else units
    across = divisor(wide, 128, 256)
    begin = column_ref[step] * wide
    for q in range(wide // across):
        source = pl.ds(pl.multiple_of(begin + q * across, 128), across)
        target = pl.ds(q * across, across)
        cot = cots[0][0, :, target]
        for j, ref in enumerate(cots[1:]):
            cot = jnp.where(step // sources == j + 1, ref[0, :, target], cot)
        for i in range(units // strip):
            at = pl.ds(i * strip, strip)
            image = dot(ht_ref[at, :], cot)
            out = image * s - a0 * v0_ref[at, source].astype(F32) - a1 * v1_ref[at, source].astype(F32)
            out_ref[at, target] = out.astype(BF16)


def final_call(column, parts, hidden_t, cots, v0, v1, scale, entries):
    units, rows = hidden_t.shape
    sources, _, wide = cots[0].shape
    features = v0.shape[1]
    vmem = pl.BlockSpec(memory_space=pltpu.VMEM)
    return pl.pallas_call(
        functools.partial(final_kernel, scale, entries, sources),
        grid_spec=pltpu.PrefetchScalarGridSpec(
            num_scalar_prefetch=1,
            grid=(len(cots) * sources,),
            in_specs=[
                pl.BlockSpec(parts.shape, lambda c, column: (0, 0, 0)),
                pl.BlockSpec((units, rows), lambda c, column: (0, 0)),
                vmem,
                vmem,
            ]
            + [pl.BlockSpec((1, rows, wide), lambda c, column: (c % sources, 0, 0))] * len(cots),
            out_specs=[
                pl.BlockSpec((units, wide), lambda c, column: (0, column[c])),
                pl.BlockSpec((1, BASIS + 1), lambda c, column: (0, 0)),
            ],
            scratch_shapes=[pltpu.SMEM((4,), F32)],
        ),
        out_shape=[
            jax.ShapeDtypeStruct((units, features), BF16),
            jax.ShapeDtypeStruct((1, BASIS + 1), F32),
        ],
        compiler_params=params(8),
        cost_estimate=pl.CostEstimate(
            flops=2 * rows * units * features, bytes_accessed=6 * units * features, transcendentals=0
        ),
        name="residual",
    )(column, parts, hidden_t, *pinned(v0, v1), *cots)


def swap(x, axis, distance):
    size = lax.axis_size(axis)
    return lax.ppermute(x, axis, [(i, i ^ distance) for i in range(size)])


def body(tokens, w_gate, w_up, basis, routes, gates, rho, sigma):
    sources, slices = lax.axis_size("dp"), lax.axis_size("slice")
    source, group, part = lax.axis_index("dp"), lax.axis_index("group"), lax.axis_index("slice")
    tok_dev, features = tokens.shape
    total = tok_dev * sources
    scale = 1.0 / math.sqrt(FF)
    kappa = E * FF / total
    entries = float(E * FF * features)
    line = sources * CAP
    rows = -(-(line + 3) // 8) * 8
    split = features % (slices * sources * 128) == 0
    cuts = slices if split else 1
    chunks = sources * cuts
    wide = features // chunks
    place = jnp.arange(chunks, dtype=jnp.int32)
    lane = part if split else 0
    column = ((place % sources) ^ source) * cuts + ((place // sources) ^ lane)
    ids = jnp.stack([source, group, column[0]]).astype(jnp.int32)
    hbm = functools.partial(pltpu.with_memory_space_constraint, memory_space=pltpu.HBM)
    w_gate, w_up, basis = hbm(w_gate), hbm(w_up), hbm(basis)

    xs = [tokens] + [swap(tokens, "dp", j) for j in range(1, sources)]
    small = hbm(routes.T), hbm(gates.T), hbm(rho[None, :]), hbm(sigma[None, :])
    wg, wu, placing, gate, rho_row, sigma_row = load_call(ids, *small, w_gate, w_up, tok_dev, rows, wide)
    hidden, v1, *tangents = hidden_call(column, xs, wg, wu, gate, placing, basis, cuts, scale)
    if split:
        got = [tangents[0]] + [swap(tangents[j], "slice", j) for j in range(1, slices)]
    else:
        got = [lax.psum(tangents[0], "slice")]
    shares = share_call(got, rho_row, line, (v1,))
    got = [shares[0]] + [swap(shares[j], "dp", j) for j in range(1, sources)]
    v0, t0, hidden_t, square = other_call(hidden, basis, shares[0], v1, chunks, scale)
    summed, rho_all = sum_call(got, rho_row, line, (v0, v1), hidden_t)
    got = [summed] + [swap(summed, "group", j) for j in range(1, E)]
    units = v0.shape[0]
    cut = units // 4 * 3
    grams = [gram_call(v0, v1, rho_all, 0, cut)]
    cot = cotangent_call(got, placing, rho_all, sigma_row, kappa, (v0, v1), grams[0])
    cots = [cot] + [swap(cot, "dp", j) for j in range(1, sources)]
    grams.append(gram_call(v0, v1, cot, cut, units))
    cots = stack_call(cots, grams[1])
    cots = [cots] + ([swap(cots, "slice", j) for j in range(1, slices)] if split else [])

    devices = sources * E * slices
    parts = products_call(column, hidden, t0, square, cots, tangents, grams, scale, devices)
    parts = lax.all_to_all(parts, EVERY, 0, 0, tiled=True)
    new, hess = final_call(column, parts, hidden_t, cots, v0, v1, scale, entries)
    return new, hess.T


def solution(mesh):
    sources, experts = mesh.shape["dp"], mesh.shape["expert"]
    fine = Mesh(mesh.devices.reshape(sources, E, experts // E), EVERY)
    units = ("group", "slice", "dp")
    return jax.shard_map(
        body,
        mesh=fine,
        in_specs=(
            P("dp", None),
            P(None, units),
            P(None, units),
            P(None, units, None),
            P(),
            P(),
            P("dp"),
            P(),
        ),
        out_specs=(P(units, None), P()),
        check_vma=False,
    )
```

```python
import functools
import math

import jax
import jax.numpy as jnp
from jax import lax
from jax.experimental import pallas as pl
from jax.experimental.pallas import tpu as pltpu
from jax.sharding import Mesh, PartitionSpec as P

FF = 8192
E = 4
BASIS = 2
STEPS = 1
CAP = 9
MIB = 1 << 20
F32 = jnp.float32
BF16 = jnp.bfloat16
EVERY = ("dp", "group", "slice")


def params(mib=None):
    return pltpu.CompilerParams(vmem_limit_bytes=mib * MIB if mib else None)


def pinned(*arrays):
    return tuple(pltpu.with_memory_space_constraint(x, pltpu.VMEM) for x in arrays)


def dot(a, b, dims=((1,), (0,))):
    return lax.dot_general(a, b, (dims, ((), ())), preferred_element_type=F32)


def divisor(total, unit, limit):
    best = unit
    for size in range(unit, limit + 1, unit):
        if total % size == 0:
            best = size
    return best


def load_kernel(tok_dev, ids_ref, routes_hbm, gates_hbm, rho_hbm, sigma_hbm, wg_hbm, wu_hbm, *outs):
    wg_ref, wu_ref, place_ref, gate_ref, rho_row_ref, sigma_row_ref = outs[:6]
    routes_ref, gates_ref, rho_ref, small_sems, w_sems = outs[6:]
    source, group, chunk = ids_ref[0], ids_ref[1], ids_ref[2]
    wide = rho_row_ref.shape[1]
    here = pl.ds(pl.multiple_of(chunk * wide, 128), wide)
    small = [
        pltpu.make_async_copy(routes_hbm, routes_ref, small_sems.at[0]),
        pltpu.make_async_copy(gates_hbm, gates_ref, small_sems.at[1]),
        pltpu.make_async_copy(rho_hbm, rho_ref, small_sems.at[2]),
        pltpu.make_async_copy(sigma_hbm.at[:, here], sigma_row_ref, small_sems.at[3]),
    ]
    depth = wg_ref.shape[0] // w_sems.shape[1]
    weights = []
    for i in range(w_sems.shape[1]):
        at = pl.ds(i * depth, depth)
        weights.append(pltpu.make_async_copy(wg_hbm.at[at], wg_ref.at[at], w_sems.at[0, i]))
        weights.append(pltpu.make_async_copy(wu_hbm.at[at], wu_ref.at[at], w_sems.at[1, i]))
    for copy in small + weights:
        copy.start()
    for copy in small:
        copy.wait()

    experts, rows, total = place_ref.shape
    routes, gates = routes_ref[...], gates_ref[...]
    first = lax.broadcasted_iota(jnp.int32, (total, total), 0)
    second = lax.broadcasted_iota(jnp.int32, (total, total), 1)
    earlier = ((first // tok_dev == second // tok_dev) & (first < second)).astype(F32).astype(BF16)
    expert = lax.broadcasted_iota(jnp.int32, (8, total), 0) ^ group
    member = jnp.zeros((8, total), F32)
    for k in range(routes.shape[0]):
        member = member + (routes[k : k + 1, :] == expert).astype(F32)
    rank = dot(member.astype(BF16), earlier).astype(jnp.int32)
    start = (lax.broadcasted_iota(jnp.int32, (8, total), 1) // tok_dev) * CAP
    slot = jnp.where(member > 0.0, start + rank, -1)
    row = lax.broadcasted_iota(jnp.int32, (rows, total), 0)
    swapped = (first // tok_dev == (second // tok_dev) ^ source) & (first % tok_dev == second % tok_dev)
    for e in range(experts):
        place = (slot[e : e + 1, :] == row).astype(F32).astype(BF16)
        place_ref[e] = dot(place, swapped.astype(F32).astype(BF16)).astype(BF16)
    gate = jnp.zeros((1, total), F32)
    for k in range(routes.shape[0]):
        gate = gate + jnp.where(routes[k : k + 1, :] == group, gates[k : k + 1, :], 0.0)
    gate_ref[...] = jnp.sum(jnp.where(swapped, gate, 0.0), axis=1, keepdims=True)
    rho_row_ref[...] = jnp.zeros_like(rho_row_ref)
    rho_row_ref[:, 0:tok_dev] = rho_ref[...]

    for copy in weights:
        copy.wait()


def load_call(ids, routes, gates, rho, sigma, w_gate, w_up, tok_dev, rows, wide):
    features, units = w_gate.shape
    total = routes.shape[1]
    vmem = pl.BlockSpec(memory_space=pltpu.VMEM)
    hbm = pl.BlockSpec(memory_space=pltpu.HBM)
    return pl.pallas_call(
        functools.partial(load_kernel, tok_dev),
        in_specs=[pl.BlockSpec(memory_space=pltpu.SMEM)] + [hbm] * 6,
        out_specs=[vmem] * 6,
        out_shape=[
            pltpu.VMEM((features, units), BF16),
            pltpu.VMEM((features, units), BF16),
            jax.ShapeDtypeStruct((E, rows, total), BF16),
            jax.ShapeDtypeStruct((total, 1), F32),
            jax.ShapeDtypeStruct((1, wide), F32),
            jax.ShapeDtypeStruct((1, wide), F32),
        ],
        scratch_shapes=[
            pltpu.VMEM(routes.shape, jnp.int32),
            pltpu.VMEM(gates.shape, F32),
            pltpu.VMEM(rho.shape, F32),
            pltpu.SemaphoreType.DMA((4,)),
            pltpu.SemaphoreType.DMA((2, features // divisor(features, 128, 1024))),
        ],
        compiler_params=params(3),
        cost_estimate=pl.CostEstimate(flops=0, bytes_accessed=8 * features * units, transcendentals=0),
        name="load",
    )(ids, routes, gates, rho, sigma, w_gate, w_up)


def vector_blocks(units):
    return 4 if units % 512 == 0 else 1


def hidden_kernel(scale, parts, cuts, column_ref, *refs):
    xs, (wg_ref, wu_ref, gate_ref, place_ref, v_hbm) = refs[:parts], refs[parts : parts + 5]
    outs = refs[parts + 5 :]
    h_ref, v_ref, tangents = outs[0], outs[1], outs[2 : 2 + cuts]
    acc_g, acc_u, v_sems = outs[2 + cuts :]
    units, features = v_ref.shape
    depth = divisor(features, 128, 1024)
    lots = [pl.ds(i * depth, depth) for i in range(features // depth)]
    height = units // v_sems.shape[0]
    bands = [pl.ds(i * height, height) for i in range(v_sems.shape[0])]
    vectors = [
        pltpu.make_async_copy(v_hbm.at[BASIS - 1, at], v_ref.at[at], v_sems.at[i]) for i, at in enumerate(bands)
    ]
    for copy in vectors:
        copy.start()

    def project(acc, w_ref):
        for i, at in enumerate(lots):
            part = dot(jnp.concatenate([ref[:, at] for ref in xs], axis=0), w_ref[at, :])
            acc[...] = acc[...] + part if i else part

    project(acc_g, wg_ref)
    project(acc_u, wu_ref)
    g = acc_g[...]
    full = (g * (1.0 / (1.0 + jnp.exp(-g))) * acc_u[...] * gate_ref[...]).astype(BF16)
    h_ref[...] = dot(place_ref[0], full).astype(BF16)

    sources, _, wide = tangents[0].shape
    for copy in vectors:
        copy.wait()
    h = h_ref[...]
    for j, out_ref in enumerate(tangents):
        for d in range(sources):
            start = pl.multiple_of(column_ref[j * sources + d] * wide, 128)
            out_ref[d] = (dot(h, v_ref[:, pl.ds(start, wide)]) * scale).astype(out_ref.dtype)


def hidden_call(column, xs, wg, wu, gate, place, basis, cuts, scale):
    _, units, features = basis.shape
    _, rows, total = place.shape
    sources = len(xs)
    wide = features // (cuts * sources)
    vmem = pl.BlockSpec(memory_space=pltpu.VMEM)
    hbm = pl.BlockSpec(memory_space=pltpu.HBM)
    return pl.pallas_call(
        functools.partial(hidden_kernel, scale, sources, cuts),
        in_specs=[pl.BlockSpec(memory_space=pltpu.SMEM)] + [vmem] * (sources + 4) + [hbm],
        out_specs=[vmem] * (2 + cuts),
        out_shape=[
            jax.ShapeDtypeStruct((rows, units), BF16),
            pltpu.VMEM((units, features), BF16),
        ]
        + [jax.ShapeDtypeStruct((sources, rows, wide), BF16 if j else F32) for j in range(cuts)],
        scratch_shapes=[
            pltpu.VMEM((total, units), F32),
            pltpu.VMEM((total, units), F32),
            pltpu.SemaphoreType.DMA((vector_blocks(units),)),
        ],
        compiler_params=params(8),
        cost_estimate=pl.CostEstimate(
            flops=6 * rows * features * units, bytes_accessed=6 * features * units, transcendentals=0
        ),
        name="hidden",
    )(column, *xs, *pinned(wg, wu), gate, place, basis)


def products_of(pairs, reads, units, features):
    strip = 32 if units % 32 == 0 else units
    wide = 256

    def fold(x):
        return jnp.sum(x.reshape(strip // 8, 8, wide), axis=0)

    def column(q, carry):
        across = pl.ds(pl.multiple_of(q * wide, 128), wide)

        def body(i, sums):
            at = pl.ds(pl.multiple_of(i * strip, strip), strip)
            values = [ref[at, across].astype(F32) for ref in reads]
            return tuple(s + fold(values[a] * values[b]) for s, (a, b) in zip(sums, pairs))

        return lax.fori_loop(0, units // strip, body, carry, unroll=4 if units // strip % 4 == 0 else 1)

    zero = jnp.zeros((8, wide), F32)
    return lax.fori_loop(0, features // wide, column, (zero,) * len(pairs))


def other_kernel(scale, h_ref, v_hbm, after_ref, held_ref, v_ref, t_ref, ht_ref, acc, sems):
    units, features = v_ref.shape
    blocks = sems.shape[0]
    depth = units // blocks
    copies = []
    for i in range(blocks):
        at = pl.ds(i * depth, depth)
        copies.append(pltpu.make_async_copy(v_hbm.at[0, at], v_ref.at[at], sems.at[i]))
    for copy in copies:
        copy.start()
    ht_ref[...] = h_ref[...].astype(F32).T.astype(BF16)
    chunks, _, wide = t_ref.shape
    for i in range(blocks):
        at = pl.ds(i * depth, depth)
        copies[i].wait()
        for c in range(chunks):
            across = pl.ds(c * wide, wide)
            part = dot(h_ref[:, at], v_ref[at, across])
            if i:
                part = part + acc[:, across]
            if i < blocks - 1:
                acc[:, across] = part
            else:
                t_ref[c] = (part * scale).astype(BF16)


def other_call(hidden, basis, after, held, chunks, scale):
    rows, units = hidden.shape
    features = basis.shape[2]
    blocks = 4 if units % 512 == 0 else 1
    vmem = pl.BlockSpec(memory_space=pltpu.VMEM)
    hbm = pl.BlockSpec(memory_space=pltpu.HBM)
    return pl.pallas_call(
        functools.partial(other_kernel, scale),
        in_specs=[vmem, hbm, hbm, vmem],
        out_specs=[vmem] * 3,
        out_shape=[
            pltpu.VMEM((units, features), BF16),
            jax.ShapeDtypeStruct((chunks, rows, features // chunks), BF16),
            jax.ShapeDtypeStruct((units, rows), BF16),
        ],
        scratch_shapes=[pltpu.VMEM((rows, features), F32), pltpu.SemaphoreType.DMA((blocks,))],
        compiler_params=params(5),
        cost_estimate=pl.CostEstimate(
            flops=2 * rows * features * units, bytes_accessed=2 * features * units, transcendentals=0
        ),
        name="other_tangent",
    )(hidden, basis, after, *pinned(held))


def gram_kernel(first, last, v0_ref, v1_ref, after_ref, out_ref):
    at = pl.ds(first, last - first)
    reads = (v0_ref.at[at], v1_ref.at[at])
    sums = products_of(((0, 0), (0, 1), (1, 1)), reads, last - first, v0_ref.shape[1])
    for n, value in enumerate(sums):
        out_ref[n] = value


def gram_call(v0, v1, after, first, last):
    vmem = pl.BlockSpec(memory_space=pltpu.VMEM)
    size = (last - first) * v0.shape[1]
    return pl.pallas_call(
        functools.partial(gram_kernel, first, last),
        in_specs=[vmem, vmem, pl.BlockSpec(memory_space=pltpu.HBM)],
        out_specs=vmem,
        out_shape=jax.ShapeDtypeStruct((3, 8, 256), F32),
        compiler_params=params(2),
        cost_estimate=pl.CostEstimate(flops=4 * size, bytes_accessed=4 * size, transcendentals=0),
        name="gram",
    )(*pinned(v0, v1), after)


def pieces(x):
    first = x.astype(BF16)
    rest = x - first.astype(F32)
    second = rest.astype(BF16)
    return first, second, (rest - second.astype(F32)).astype(BF16)


def share_kernel(line, parts, *refs):
    ins, rho_ref, outs = refs[:parts], refs[parts], refs[parts + 2 :]
    rows, wide = ins[0].shape[1:]
    row = lax.broadcasted_iota(jnp.int32, (rows, wide), 0)
    for j, out_ref in enumerate(outs):
        total = ins[0][j].astype(F32)
        for ref in ins[1:]:
            total = total + ref[j].astype(F32)
        if j:
            for n, piece in enumerate(pieces(rho_ref[...])):
                total = jnp.where(row == line + n, piece.astype(F32), total)
        out_ref[...] = total.astype(out_ref.dtype)


def share_call(parts, rho_row, line, held):
    sources, rows, wide = parts[0].shape
    return pl.pallas_call(
        functools.partial(share_kernel, line, len(parts)),
        in_specs=[pl.BlockSpec(memory_space=pltpu.VMEM)] * (len(parts) + 2),
        out_shape=[jax.ShapeDtypeStruct((rows, wide), BF16 if j else F32) for j in range(sources)],
        compiler_params=params(6),
        name="slice_sum",
    )(*parts, rho_row, *pinned(*held))


def sum_kernel(line, *refs):
    ins, rho_own, out_ref, rho_ref = refs[:-6], refs[-6], refs[-2], refs[-1]
    total = ins[0][...]
    rho_ref[0:1, :] = rho_own[:, 0:128]
    for j, ref in enumerate(ins[1:]):
        part = ref[...].astype(F32)
        total = total + part
        rho_ref[j + 1 : j + 2, :] = (
            part[line : line + 1, 0:128] + part[line + 1 : line + 2, 0:128] + part[line + 2 : line + 3, 0:128]
        )
    row = lax.broadcasted_iota(jnp.int32, total.shape, 0)
    out_ref[...] = jnp.where(row < line, total, 0.0).astype(BF16)


def sum_call(parts, rho_row, line, held, after):
    rows, wide = parts[0].shape
    return pl.pallas_call(
        functools.partial(sum_kernel, line),
        in_specs=[pl.BlockSpec(memory_space=pltpu.VMEM)] * (len(parts) + 4),
        out_shape=[
            jax.ShapeDtypeStruct((rows, wide), BF16),
            jax.ShapeDtypeStruct((len(parts), 128), F32),
        ],
        compiler_params=params(6),
        name="plane_sum",
    )(*parts, rho_row, *pinned(*held), after)


def cotangent_kernel(parts, kappa, place_ref, rho_ref, sigma_ref, *refs):
    ins, out_ref = refs[:parts], refs[-1]
    response = None
    for j, ref in enumerate(ins):
        term = dot(place_ref[j], ref[...], ((0,), (0,)))
        response = term if response is None else response + term
    sources, tok_dev = rho_ref.shape[0], response.shape[0] // rho_ref.shape[0]
    down = lax.broadcasted_iota(jnp.int32, (tok_dev, 128), 0)
    across = lax.broadcasted_iota(jnp.int32, (tok_dev, 128), 1)
    columns = [
        jnp.sum(jnp.where(down == across, rho_ref[j : j + 1, :], 0.0), axis=1, keepdims=True)
        for j in range(sources)
    ]
    rho = jnp.concatenate(columns, axis=0)
    cot = (kappa * rho * sigma_ref[...] * response).astype(BF16)
    out_ref[...] = dot(place_ref[0], cot).astype(BF16)


def cotangent_call(parts, placing, rho_all, sigma_row, kappa, held, after):
    return pl.pallas_call(
        functools.partial(cotangent_kernel, len(parts), kappa),
        in_specs=[pl.BlockSpec(memory_space=pltpu.VMEM)] * (len(parts) + 6),
        out_shape=jax.ShapeDtypeStruct(parts[0].shape, BF16),
        compiler_params=params(6),
        name="cotangent",
    )(placing, rho_all, sigma_row, *parts, *pinned(*held), after)


def stack_kernel(*refs):
    for j, ref in enumerate(refs[:-2]):
        refs[-1][j] = ref[...]


def stack_call(parts, after):
    return pl.pallas_call(
        stack_kernel,
        in_specs=[pl.BlockSpec(memory_space=pltpu.VMEM)] * (len(parts) + 1),
        out_specs=pl.BlockSpec(memory_space=pltpu.VMEM),
        out_shape=jax.ShapeDtypeStruct((len(parts),) + parts[0].shape, parts[0].dtype),
        compiler_params=params(6),
        name="stack",
    )(*parts, after)


def products_kernel(scale, cuts, column_ref, h_ref, t0_ref, *refs):
    out_ref = refs[-1]
    cots, tangents, grams = refs[:cuts], refs[cuts : 2 * cuts], refs[2 * cuts : -1]
    sources, rows, wide = cots[0].shape
    h = h_ref[...]
    weight = dot(h, h, ((1,), (1,)))
    c0 = jnp.zeros((rows, wide), F32)
    c1 = jnp.zeros((rows, wide), F32)
    square = jnp.zeros((rows, rows), F32)
    for j in range(cuts):
        for d in range(sources):
            cot = cots[j][d]
            value = cot.astype(F32)
            c0 = c0 + value * t0_ref[column_ref[j * sources + d]].astype(F32)
            c1 = c1 + value * tangents[j][d].astype(F32)
            square = square + dot(cot, cot, ((1,), (1,)))
    values = (
        jnp.sum(c0),
        jnp.sum(c1),
        jnp.sum(weight * square) * (scale * scale),
        jnp.sum(sum(ref[0] for ref in grams)),
        jnp.sum(sum(ref[1] for ref in grams)),
        jnp.sum(sum(ref[2] for ref in grams)),
    )
    lane = lax.broadcasted_iota(jnp.int32, out_ref.shape, 2)
    out = jnp.zeros(out_ref.shape, F32)
    for n, value in enumerate(values):
        out = jnp.where(lane == n, value, out)
    out_ref[...] = out


def products_call(column, hidden, t0, cots, tangents, grams, scale, devices):
    vmem = pl.BlockSpec(memory_space=pltpu.VMEM)
    args = (hidden, t0, *cots, *tangents, *grams)
    return pl.pallas_call(
        functools.partial(products_kernel, scale, len(cots)),
        in_specs=[pl.BlockSpec(memory_space=pltpu.SMEM)] + [vmem] * len(args),
        out_specs=vmem,
        out_shape=jax.ShapeDtypeStruct((devices, 1, 128), F32),
        compiler_params=params(8),
        name="products",
    )(column, *args)


def final_kernel(scale, entries, sources, column_ref, parts_ref, ht_ref, v0_ref, v1_ref, *refs):
    cots, (out_ref, hess_ref, scalars) = refs[:-3], refs[-3:]
    step = pl.program_id(0)

    @pl.when(step == 0)
    def _():
        total = jnp.sum(parts_ref[...], axis=0) * (1.0 / entries)
        c0, c1, square = total[:, 0:1], total[:, 1:2], total[:, 2:3]
        g00, g01, g11 = total[:, 3:4], total[:, 4:5], total[:, 5:6]
        norm = square - 2.0 * (c0 * c0 + c1 * c1) + c0 * c0 * g00 + 2.0 * c0 * c1 * g01 + c1 * c1 * g11
        beta = jnp.sqrt(jnp.maximum(norm, square * 2.0**-24))
        lane = lax.broadcasted_iota(jnp.int32, hess_ref.shape, 1)
        hess_ref[...] = jnp.where(lane == 0, c0, jnp.where(lane == 1, c1, beta))
        inverse = 1.0 / beta
        scalars[0] = (c0 * inverse)[0, 0]
        scalars[1] = (c1 * inverse)[0, 0]
        scalars[2] = (scale * inverse)[0, 0]

    a0, a1, s = scalars[0], scalars[1], scalars[2]
    units, wide = out_ref.shape
    strip = 256 if units % 256 == 0 else units
    across = divisor(wide, 128, 256)
    begin = column_ref[step] * wide
    for q in range(wide // across):
        source = pl.ds(pl.multiple_of(begin + q * across, 128), across)
        target = pl.ds(q * across, across)
        cot = cots[0][0, :, target]
        for j, ref in enumerate(cots[1:]):
            cot = jnp.where(step // sources == j + 1, ref[0, :, target], cot)
        for i in range(units // strip):
            at = pl.ds(i * strip, strip)
            image = dot(ht_ref[at, :], cot)
            out = image * s - a0 * v0_ref[at, source].astype(F32) - a1 * v1_ref[at, source].astype(F32)
            out_ref[at, target] = out.astype(BF16)


def final_call(column, parts, hidden_t, cots, v0, v1, scale, entries):
    units, rows = hidden_t.shape
    sources, _, wide = cots[0].shape
    features = v0.shape[1]
    vmem = pl.BlockSpec(memory_space=pltpu.VMEM)
    return pl.pallas_call(
        functools.partial(final_kernel, scale, entries, sources),
        grid_spec=pltpu.PrefetchScalarGridSpec(
            num_scalar_prefetch=1,
            grid=(len(cots) * sources,),
            in_specs=[
                pl.BlockSpec(parts.shape, lambda c, column: (0, 0, 0)),
                pl.BlockSpec((units, rows), lambda c, column: (0, 0)),
                vmem,
                vmem,
            ]
            + [pl.BlockSpec((1, rows, wide), lambda c, column: (c % sources, 0, 0))] * len(cots),
            out_specs=[
                pl.BlockSpec((units, wide), lambda c, column: (0, column[c])),
                pl.BlockSpec((1, BASIS + 1), lambda c, column: (0, 0)),
            ],
            scratch_shapes=[pltpu.SMEM((4,), F32)],
        ),
        out_shape=[
            jax.ShapeDtypeStruct((units, features), BF16),
            jax.ShapeDtypeStruct((1, BASIS + 1), F32),
        ],
        compiler_params=params(8),
        cost_estimate=pl.CostEstimate(
            flops=2 * rows * units * features, bytes_accessed=6 * units * features, transcendentals=0
        ),
        name="residual",
    )(column, parts, hidden_t, *pinned(v0, v1), *cots)


def swap(x, axis, distance):
    size = lax.axis_size(axis)
    return lax.ppermute(x, axis, [(i, i ^ distance) for i in range(size)])


def body(tokens, w_gate, w_up, basis, routes, gates, rho, sigma):
    sources, slices = lax.axis_size("dp"), lax.axis_size("slice")
    source, group, part = lax.axis_index("dp"), lax.axis_index("group"), lax.axis_index("slice")
    tok_dev, features = tokens.shape
    total = tok_dev * sources
    scale = 1.0 / math.sqrt(FF)
    kappa = E * FF / total
    entries = float(E * FF * features)
    line = sources * CAP
    rows = -(-(line + 3) // 8) * 8
    split = features % (slices * sources * 128) == 0
    cuts = slices if split else 1
    chunks = sources * cuts
    wide = features // chunks
    place = jnp.arange(chunks, dtype=jnp.int32)
    lane = part if split else 0
    column = ((place % sources) ^ source) * cuts + ((place // sources) ^ lane)
    ids = jnp.stack([source, group, column[0]]).astype(jnp.int32)
    hbm = functools.partial(pltpu.with_memory_space_constraint, memory_space=pltpu.HBM)
    w_gate, w_up, basis = hbm(w_gate), hbm(w_up), hbm(basis)

    xs = [tokens] + [swap(tokens, "dp", j) for j in range(1, sources)]
    small = hbm(routes.T), hbm(gates.T), hbm(rho[None, :]), hbm(sigma[None, :])
    wg, wu, placing, gate, rho_row, sigma_row = load_call(ids, *small, w_gate, w_up, tok_dev, rows, wide)
    hidden, v1, *tangents = hidden_call(column, xs, wg, wu, gate, placing, basis, cuts, scale)
    if split:
        got = [tangents[0]] + [swap(tangents[j], "slice", j) for j in range(1, slices)]
    else:
        got = [lax.psum(tangents[0], "slice")]
    shares = share_call(got, rho_row, line, (v1,))
    got = [shares[0]] + [swap(shares[j], "dp", j) for j in range(1, sources)]
    v0, t0, hidden_t = other_call(hidden, basis, shares[0], v1, chunks, scale)
    summed, rho_all = sum_call(got, rho_row, line, (v0, v1), hidden_t)
    got = [summed] + [swap(summed, "group", j) for j in range(1, E)]
    units = v0.shape[0]
    cut = units * 5 // 8 // 32 * 32
    grams = [gram_call(v0, v1, rho_all, 0, cut)]
    cot = cotangent_call(got, placing, rho_all, sigma_row, kappa, (v0, v1), grams[0])
    cots = [cot] + [swap(cot, "dp", j) for j in range(1, sources)]
    grams.append(gram_call(v0, v1, cot, cut, units))
    cots = stack_call(cots, grams[1])
    cots = [cots] + ([swap(cots, "slice", j) for j in range(1, slices)] if split else [])

    devices = sources * E * slices
    parts = products_call(column, hidden, t0, cots, tangents, grams, scale, devices)
    parts = lax.all_to_all(parts, EVERY, 0, 0, tiled=True)
    new, hess = final_call(column, parts, hidden_t, cots, v0, v1, scale, entries)
    return new, hess.T


def solution(mesh):
    sources, experts = mesh.shape["dp"], mesh.shape["expert"]
    fine = Mesh(mesh.devices.reshape(sources, E, experts // E), EVERY)
    units = ("group", "slice", "dp")
    return jax.shard_map(
        body,
        mesh=fine,
        in_specs=(
            P("dp", None),
            P(None, units),
            P(None, units),
            P(None, units, None),
            P(),
            P(),
            P("dp"),
            P(),
        ),
        out_specs=(P(units, None), P()),
        check_vma=False,
    )
```
